128 devices in a mesh: gx: 8 (over z_lo, y), gy: 16 (over z_hi, x, core).
Axes of the slice: x: 4, y: 4, z: 4 (z_hi: 2, z_lo: 2; z = z_hi * 2 + z_lo), core: 2. Of those that a mesh axis runs over, the one named last changes fastest.
Arguments:
- thermal_rows: float32 [196608, 128], P(('gx', 'gy')), may hold values from -6 to 6
- row_owner: int32 [196608, 1], P(('gx', 'gy')), may hold values from 0 to 127; in each aligned block of 1536 rows (0 to 1535, 1536 to 3071, ...) at most 24 rows name the same one
- row_element: int32 [196608, 1], P(('gx', 'gy')), may hold values from 0 to 1023
- modulus: float32 [64, 128, 2048], P(None, 'gx', 'gy'), may hold values from 0.5 to 5
- birth: int32 [64, 128, 2048], P(None, 'gx', 'gy'), may hold values from 0 to 4
- start_disp: float32 [3, 64, 128, 2048], P(None, None, 'gx', 'gy'), may hold values from -6 to 6
- bounds: float32 [2], replicated, as said below
Outputs:
- displacement: float32 [3, 64, 128, 2048], P(None, None, 'gx', 'gy')
The draws below stay inside these ranges and needn't reach their ends.
Inputs may be any that keep to these rules, and one draw needn't show every extreme that they name: `row_owner`: no device holds more than 24 rows for one tile, and some device holds exactly 24 rows for some tile. `bounds`: 0 < lo < hi.
All inputs are finite; a program needn't handle non-finite values.
Results may differ from the reference program's by a relative error of at most 0.00002.
Values sent between devices are 32-bit elements; how exact they have to be, the bound alone decides.
A program may use at most 192 MiB of HBM per device.

```python
import math
import jax
import jax.numpy as jnp
import numpy as np
from jax import lax

NZ = 64
CX = 16
CY = 128
SWEEPS = 4
CAP = 24
R_DEV = 1536
ROWS = 196608
NX = 128
NY = 2048
N_GX = 8
N_GY = 16


def draw_bounds(key, part):
    key = jax.random.fold_in(key, 7)
    upper = jax.random.uniform(key, (), jnp.float32, 1.9, 2.3)
    spread = jax.random.uniform(jax.random.fold_in(key, 1), (), jnp.float32, 0.05, 0.3)
    return jnp.stack([upper * spread, upper]).astype(jnp.float32)


def place_ends(array, own_key, smallest, top_value):
    spot = [jax.random.randint(jax.random.fold_in(own_key, axis), (), 0, length) for axis, length in enumerate(array.shape)]
    main_axis = array.shape.index(max(array.shape))
    beside = spot[:main_axis] + [(spot[main_axis] + 1) % array.shape[main_axis]] + spot[main_axis + 1:]
    return array.at[tuple(spot)].set(smallest).at[tuple(beside)].set(top_value)


def steps_of(key, dims, split, low, top_value):
    loudness = 1.0
    for axis_at, shards_of in split:
        heights = jax.random.uniform(jax.random.fold_in(jax.random.fold_in(key, 6), axis_at), (shards_of,), jnp.float32, low / len(split), top_value / len(split))
        loudness = loudness * jnp.repeat(jnp.exp(heights), dims[axis_at] // shards_of).reshape((-1,) + (1,) * (len(dims) - 1 - axis_at))
    return loudness


def routed_block(key, own, number, rows, amount, top, bound, skew):
    ranking = jax.random.permutation(key, amount)
    packed, common = portions_of(amount, rows * top, bound, skew, True), portions_of(amount, rows * top, bound, skew, False)
    places = jnp.arange(amount)

    def named(sizes, turn):
        used = int((sizes > 0).sum())
        fixed = max(1, used // 4)
        moved = fixed + (places - fixed + turn * (used - fixed)) % max(1, amount - fixed)
        return jnp.zeros((amount,), jnp.int32).at[ranking[jnp.where(places < fixed, places, moved)]].set(jnp.asarray(sizes, jnp.int32))

    sizes = jnp.where(number % 4 == 0, named(packed, number // 4), named(common, number - number // 4 - 1))
    mixed = jax.random.permutation(jax.random.fold_in(own, 3), amount)
    donor, taker = mixed[0:amount // 2 * 2:2], mixed[1:amount // 2 * 2:2]
    room = jnp.minimum(sizes[donor] - 1, bound - sizes[taker]) // 2
    room = jnp.where((donor == ranking[0]) | (taker == ranking[0]) | (sizes[taker] == 0), 0, jnp.maximum(room, 0))
    moved = jax.random.randint(jax.random.fold_in(own, 4), (amount // 2,), 0, 1 << 20) % (room + 1)
    sizes = sizes.at[donor].add(-moved).at[taker].add(moved)
    labels = jnp.searchsorted(jnp.cumsum(sizes), jnp.arange(rows * top), side="right").astype(jnp.int32)
    table = labels.reshape(top, rows).T
    table = table[jax.random.permutation(jax.random.fold_in(own, 1), rows)]
    turn = jax.random.randint(jax.random.fold_in(own, 2), (rows, 1), 0, top)
    return jnp.take_along_axis(table, (jnp.arange(top)[None, :] + turn) % top, axis=1)


def portions_of(amount, total, most, slope, full):
    portions = [(1 << 20) // math.isqrt(rank ** slope) + 1 for rank in range(1, amount + 1)]
    largest = most if full else min(most, max(-(-total // amount), total * portions[0] // sum(portions)))
    least = 1 if total - largest >= amount - 1 else 0
    counts, surplus = [largest] + [least] * (amount - 1), total - largest - least * (amount - 1)
    while surplus > 0:
        candidates = [i for i in range(1, amount) if counts[i] < largest] or [i for i in range(1, amount) if counts[i] < most]
        whole, budget = sum([portions[i] for i in candidates]), surplus
        for i in candidates:
            addition = min(most - counts[i], max(1, budget * portions[i] // whole), surplus)
            counts[i] = counts[i] + addition
            surplus = surplus - addition
    return np.array(counts)


def gaussian(stream_key, shape, scale, bound, split=(), kind=jnp.bfloat16):
    drawn = scale * jax.random.normal(stream_key, shape, jnp.float32)
    if split:
        drawn = drawn * steps_of(stream_key, shape, split, -0.22, 0.18)
    return jnp.clip(drawn, -bound, bound).astype(kind)


def setup_inputs(seed: int = 0) -> dict:
    splits = jax.random.split(jax.random.key(seed), 8)
    thermal_rows = gaussian(splits[0], (ROWS, CY), 1.0, 6.0, ((0, 128),), jnp.float32)
    row_owner_keys = jax.random.split(jax.random.fold_in(splits[1], 1), ROWS // R_DEV)
    row_owner_turns = jax.random.permutation(jax.random.fold_in(splits[1], 3), ROWS // R_DEV)
    row_owner = jax.vmap(lambda own, number: routed_block(jax.random.fold_in(splits[1], 2), own, number, R_DEV, N_GX * N_GY, 1, CAP, 2))(row_owner_keys, row_owner_turns).reshape((ROWS, 1))
    row_element = place_ends(jax.random.randint(splits[2], (ROWS, 1), 0, NZ * CX), jax.random.fold_in(splits[2], 1), 0, (NZ * CX) - 1).astype(jnp.int32)
    modulus = jnp.clip(jnp.exp(math.log(5.0) - 2.3025851 * jax.random.uniform(splits[3], (NZ, NX, NY), jnp.float32) ** steps_of(splits[3], (NZ, NX, NY), ((1, 8), (2, 16)), -0.2, 0.2)), 0.5, 5.0)
    birth = place_ends(jax.random.randint(splits[4], (NZ, NX, NY), 0, SWEEPS + 1), jax.random.fold_in(splits[4], 1), 0, SWEEPS).astype(jnp.int32)
    start_disp = gaussian(splits[5], (3, NZ, NX, NY), 1.0, 6.0, ((2, 8), (3, 16)), jnp.float32)
    bounds = draw_bounds(jax.random.fold_in(splits[7], 71), 0)
    return dict(thermal_rows=thermal_rows, row_owner=row_owner, row_element=row_element, modulus=modulus, birth=birth, start_disp=start_disp, bounds=bounds)


NEIGHBOUR_WEIGHTS = (0.0, 1.0, 0.5, 0.25)
DIAGONAL_WEIGHT = 14.5
COUPLING = 0.25
SOFTENED = 0.05


def operate(padded, modulus_now):
    depth = padded.shape[1] - 2
    breadth = padded.shape[2] - 2
    length = padded.shape[3] - 2

    def neighbour(a, b, c):
        return padded[:, 1 + a:1 + a + depth, 1 + b:1 + b + breadth, 1 + c:1 + c + length]

    middle = neighbour(0, 0, 0)
    beside_all = jnp.zeros_like(middle)
    for a in (-1, 0, 1):
        for b in (-1, 0, 1):
            for c in (-1, 0, 1):
                distance = abs(a) + abs(b) + abs(c)
                if distance:
                    beside_all = beside_all + NEIGHBOUR_WEIGHTS[distance] * neighbour(a, b, c)
    unit_steps = ((1, 0, 0), (0, 1, 0), (0, 0, 1))
    coupled = []
    for component in range(3):
        summed = jnp.zeros_like(middle[0])
        for second in range(3):
            if second != component:
                e = unit_steps[component]
                f = unit_steps[second]
                plus_plus = neighbour(e[0] + f[0], e[1] + f[1], e[2] + f[2])[second]
                plus_minus = neighbour(e[0] - f[0], e[1] - f[1], e[2] - f[2])[second]
                minus_plus = neighbour(f[0] - e[0], f[1] - e[1], f[2] - e[2])[second]
                minus_minus = neighbour(-e[0] - f[0], -e[1] - f[1], -e[2] - f[2])[second]
                summed = summed + 0.25 * (plus_plus - plus_minus - minus_plus + minus_minus)
        coupled.append(summed)
    return modulus_now * (DIAGONAL_WEIGHT * middle - beside_all - COUPLING * jnp.stack(coupled))


def load_from(padded_stress):
    along_z = 0.5 * (padded_stress[2:, 1:-1, 1:-1] - padded_stress[:-2, 1:-1, 1:-1])
    along_x = 0.5 * (padded_stress[1:-1, 2:, 1:-1] - padded_stress[1:-1, :-2, 1:-1])
    along_y = 0.5 * (padded_stress[1:-1, 1:-1, 2:] - padded_stress[1:-1, 1:-1, :-2])
    return jnp.stack([along_z, along_x, along_y])


def apply_whole(field, modulus_now):
    padded = jnp.pad(field, ((0, 0), (1, 1), (1, 1), (1, 1)))

    def block(index):
        start = index * CX
        slab = lax.dynamic_slice_in_dim(padded, start, CX + 2, 2)
        modulus_slab = lax.dynamic_slice_in_dim(modulus_now, start, CX, 1)
        return operate(slab, modulus_slab)

    blocks = lax.map(block, jnp.arange(N_GX, dtype=jnp.int32))
    return jnp.transpose(blocks, (1, 2, 0, 3, 4)).reshape(3, NZ, NX, NY)


def reference(thermal_rows, row_owner, row_element, modulus, birth, start_disp, bounds):
    owner = row_owner[:, 0]
    element = row_element[:, 0]
    depth_index = element // CX
    local_x = element % CX
    tile_x = owner // N_GY
    tile_y = owner % N_GY
    keys = ((depth_index * NX + tile_x * CX + local_x) * N_GY + tile_y).astype(jnp.int32)
    summed_rows = jax.ops.segment_sum(thermal_rows, keys, num_segments=NZ * NX * N_GY)
    increment = summed_rows.reshape(NZ, NX, NY)
    stress = modulus * increment
    load = load_from(jnp.pad(stress, 1))
    lower = bounds[0]
    upper = bounds[1]
    theta = (upper + lower) / 2.0
    delta = (upper - lower) / 2.0
    sigma = theta / delta
    ratio_now = 1.0 / sigma
    field = start_disp
    step_field = jnp.zeros_like(field)
    for sweep in range(SWEEPS):
        active = modulus * jnp.where(birth <= sweep, 1.0, SOFTENED).astype(jnp.float32)
        residual = load - apply_whole(field, active)
        scaled = residual / (DIAGONAL_WEIGHT * active)
        if sweep == 0:
            step_field = scaled / theta
        else:
            ratio_next = 1.0 / (2.0 * sigma - ratio_now)
            step_field = ratio_next * ratio_now * step_field + (2.0 * ratio_next / delta) * scaled
            ratio_now = ratio_next
        field = field + step_field
    return field
```

```python
import functools

import jax
import jax.numpy as jnp
from jax import lax
from jax.experimental import pallas as pl
from jax.experimental.pallas import tpu as pltpu
from jax.sharding import PartitionSpec as P

SWEEPS = 4
CAP = 24


NEIGHBOUR_WEIGHTS = (0.0, 1.0, 0.5, 0.25)
DIAGONAL_WEIGHT = 14.5
COUPLING = 0.25
SOFTENED = 0.05


def with_halo(cells, sides, width):
    for axis, dim in sides:
        count = lax.axis_size(axis)
        ends = count - 1
        head = lax.slice_in_dim(cells, 0, width, axis=dim)
        tail = lax.slice_in_dim(cells, cells.shape[dim] - width, cells.shape[dim], axis=dim)
        cells = jnp.concatenate(
            [
                lax.ppermute(tail, axis, [(i, (i + 1) % count) for i in range(ends)]),
                cells,
                lax.ppermute(head, axis, [((i + 1) % count, i) for i in range(ends)]),
            ],
            axis=dim,
        )
    return cells


def operate(padded, modulus_now):
    depth = padded.shape[1] - 2
    breadth = padded.shape[2] - 2
    length = padded.shape[3] - 2

    def neighbour(a, b, c):
        return padded[:, 1 + a : 1 + a + depth, 1 + b : 1 + b + breadth, 1 + c : 1 + c + length]

    middle = neighbour(0, 0, 0)
    beside_all = jnp.zeros_like(middle)
    for a in (-1, 0, 1):
        for b in (-1, 0, 1):
            for c in (-1, 0, 1):
                distance = abs(a) + abs(b) + abs(c)
                if distance:
                    beside_all = beside_all + NEIGHBOUR_WEIGHTS[distance] * neighbour(a, b, c)
    unit_steps = ((1, 0, 0), (0, 1, 0), (0, 0, 1))
    coupled = []
    for component in range(3):
        summed = jnp.zeros_like(middle[0])
        for second in range(3):
            if second != component:
                e = unit_steps[component]
                f = unit_steps[second]
                plus_plus = neighbour(e[0] + f[0], e[1] + f[1], e[2] + f[2])[second]
                plus_minus = neighbour(e[0] - f[0], e[1] - f[1], e[2] - f[2])[second]
                minus_plus = neighbour(f[0] - e[0], f[1] - e[1], f[2] - e[2])[second]
                minus_minus = neighbour(-e[0] - f[0], -e[1] - f[1], -e[2] - f[2])[second]
                summed = summed + 0.25 * (plus_plus - plus_minus - minus_plus + minus_minus)
        coupled.append(summed)
    return modulus_now * (DIAGONAL_WEIGHT * middle - beside_all - COUPLING * jnp.stack(coupled))


def load_from(padded_stress):
    along_z = 0.5 * (padded_stress[2:, 1:-1, 1:-1] - padded_stress[:-2, 1:-1, 1:-1])
    along_x = 0.5 * (padded_stress[1:-1, 2:, 1:-1] - padded_stress[1:-1, :-2, 1:-1])
    along_y = 0.5 * (padded_stress[1:-1, 1:-1, 2:] - padded_stress[1:-1, 1:-1, :-2])
    return jnp.stack([along_z, along_x, along_y])


def padded_field(field):
    extended = with_halo(field, (("gx", 2), ("gy", 3)), 1)
    return jnp.pad(extended, ((0, 0), (1, 1), (0, 0), (0, 0)))


def advance(step_prev, scaled, sweep, ratio_now, sigma, delta, theta):
    if sweep == 0:
        return (scaled / theta, ratio_now)
    ratio_next = 1.0 / (2.0 * sigma - ratio_now)
    return (ratio_next * ratio_now * step_prev + 2.0 * ratio_next / delta * scaled, ratio_next)

MESH = pl.DeviceIdType.MESH


def halves(values):
    high = values.astype(jnp.bfloat16)
    low = (values - high.astype(jnp.float32)).astype(jnp.bfloat16)
    return high, low


def onehot(matches):
    return jnp.where(matches, 1.0, 0.0).astype(jnp.bfloat16)


def exchange_kernel(
    nx, ny, owner_ref, element_ref, rows_ref, out_ref,
    split_ref, place_ref, send_rows, send_ids, got_rows, got_ids, total,
    ids_send_sem, ids_recv_sem, rows_send_sem, rows_recv_sem,
):
    tiles = nx * ny
    count = rows_ref.shape[0]
    length = rows_ref.shape[1]
    elements = out_ref.shape[0]
    group = ny * CAP
    gx = lax.axis_index("gx")
    gy = lax.axis_index("gy")

    def there(step):
        return lax.rem(gx + step // ny, nx), lax.rem(gy + lax.rem(step, ny), ny)

    barrier = pltpu.get_barrier_semaphore()

    def greet(step, carry):
        pl.semaphore_signal(barrier, inc=1, device_id=there(step), device_id_type=MESH)
        return carry

    lax.fori_loop(1, tiles, greet, 0)

    owner = owner_ref[...]
    element = element_ref[...] + 1
    tile_of = lax.broadcasted_iota(jnp.int32, (tiles, count), 0)
    member = jnp.where(tile_of == owner, 1.0, 0.0)
    member16 = member.astype(jnp.bfloat16)
    block = 256
    earlier = onehot(
        lax.broadcasted_iota(jnp.int32, (block, block), 0) < lax.broadcasted_iota(jnp.int32, (block, block), 1)
    )
    carry = jnp.zeros((tiles, 1), jnp.float32)
    slots = []
    for first in range(0, count, block):
        part = member[:, first : first + block]
        before = jnp.dot(member16[:, first : first + block], earlier, preferred_element_type=jnp.float32) + carry
        slots.append(jnp.sum(before * part, axis=0, keepdims=True))
        carry = carry + jnp.sum(part, axis=1, keepdims=True)
    slot = jnp.concatenate(slots, axis=1).astype(jnp.int32)
    place_ref[...] = owner * CAP + slot

    weighed = jnp.concatenate(
        [
            (member * (element // 32).astype(jnp.float32)).astype(jnp.bfloat16),
            (member * lax.rem(element, 32).astype(jnp.float32)).astype(jnp.bfloat16),
        ],
        axis=0,
    )
    slot_of = onehot(lax.broadcasted_iota(jnp.int32, (length, count), 0) == slot)
    both = lax.dot_general(weighed, slot_of, (((1,), (1,)), ((), ())), preferred_element_type=jnp.float32)
    send_ids[...] = (32.0 * both[:tiles] + both[tiles:]).reshape(tiles, 1, length)

    high, low = halves(rows_ref[...])
    split_ref[:, :length] = high
    split_ref[:, length:] = low

    pl.semaphore_wait(barrier, tiles - 1)

    def number(device):
        return device[0] * ny + device[1]

    def send_id(step, carry):
        to = there(step)
        pltpu.make_async_remote_copy(
            src_ref=send_ids.at[number(to)],
            dst_ref=got_ids.at[step],
            send_sem=ids_send_sem,
            recv_sem=ids_recv_sem,
            device_id=to,
            device_id_type=MESH,
        ).start()
        return carry

    lax.fori_loop(1, tiles, send_id, 0)
    got_ids[0] = send_ids[number((gx, gy))]

    def pack(turn, carry):
        tile_x = lax.rem(gx + turn, nx)
        base = tile_x * group
        wanted = base + lax.broadcasted_iota(jnp.int32, (group, count), 0)
        pick = onehot(wanted == place_ref[...])
        picked = jnp.dot(pick, split_ref[...], preferred_element_type=jnp.float32)
        packed = (picked[:, :length] + picked[:, length:]).reshape(ny, CAP, length)
        send_rows[pl.ds(tile_x * ny, ny)] = packed

        def send(turn_y, carry):
            tile_y = lax.rem(gy + turn_y, ny)
            pltpu.make_async_remote_copy(
                src_ref=send_rows.at[tile_x * ny + tile_y],
                dst_ref=got_rows.at[turn * ny + turn_y],
                send_sem=rows_send_sem,
                recv_sem=rows_recv_sem.at[turn],
                device_id=(tile_x, tile_y),
                device_id_type=MESH,
            ).start()
            return carry

        @pl.when(turn == 0)
        def _():
            lax.fori_loop(1, ny, send, 0)

        @pl.when(turn > 0)
        def _():
            lax.fori_loop(0, ny, send, 0)

        return carry

    lax.fori_loop(0, nx, pack, 0)
    got_rows[0] = send_rows[number((gx, gy))]

    rest = pl.ds(1, tiles - 1)
    pltpu.make_async_copy(got_ids.at[rest], got_ids.at[rest], ids_recv_sem).wait()

    spread = onehot(
        lax.broadcasted_iota(jnp.int32, (length, group), 0)
        == lax.rem(lax.broadcasted_iota(jnp.int32, (length, group), 1), CAP)
    )
    own_lane = lax.broadcasted_iota(jnp.int32, (ny, group), 0) == lax.broadcasted_iota(jnp.int32, (ny, group), 1) // CAP
    total[...] = jnp.zeros_like(total)

    def collect(turn, carry):
        @pl.when(turn == 0)
        def _():
            part = got_rows.at[pl.ds(1, ny - 1)]
            pltpu.make_async_copy(part, part, rows_recv_sem.at[0]).wait()

        @pl.when(turn > 0)
        def _():
            part = got_rows.at[pl.ds(turn * ny, ny)]
            pltpu.make_async_copy(part, part, rows_recv_sem.at[turn]).wait()

        ids = got_ids[pl.ds(turn * ny, ny)].reshape(ny, length)
        ids_high = jnp.floor(ids * (1.0 / 32.0))
        ids_low = ids - 32.0 * ids_high
        wide = 32.0 * jnp.dot(ids_high.astype(jnp.bfloat16), spread, preferred_element_type=jnp.float32) + jnp.dot(
            ids_low.astype(jnp.bfloat16), spread, preferred_element_type=jnp.float32
        )
        flat = jnp.sum(jnp.where(own_lane, wide, 0.0), axis=0, keepdims=True).astype(jnp.int32) - 1
        place = onehot(lax.broadcasted_iota(jnp.int32, (elements, group), 0) == flat)
        high, low = halves(got_rows[pl.ds(turn * ny, ny)].reshape(group, length))
        total[...] += jnp.dot(place, jnp.concatenate([high, low], axis=1), preferred_element_type=jnp.float32)
        return carry

    lax.fori_loop(0, nx, collect, 0)
    out_ref[...] = total[:, :length] + total[:, length:]

    pltpu.make_async_copy(send_ids.at[rest], send_ids.at[rest], ids_send_sem).wait()
    pltpu.make_async_copy(send_rows.at[rest], send_rows.at[rest], rows_send_sem).wait()


def exchange(owner, element, rows, elements):
    nx, ny = lax.axis_size("gx"), lax.axis_size("gy")
    tiles = nx * ny
    count, length = rows.shape
    return pl.pallas_call(
        functools.partial(exchange_kernel, nx, ny),
        out_shape=jax.ShapeDtypeStruct((elements, length), jnp.float32),
        in_specs=[pl.BlockSpec(memory_space=pltpu.VMEM)] * 3,
        out_specs=pl.BlockSpec(memory_space=pltpu.VMEM),
        scratch_shapes=[
            pltpu.VMEM((count, 2 * length), jnp.bfloat16),
            pltpu.VMEM((1, count), jnp.int32),
            pltpu.VMEM((tiles, CAP, length), jnp.float32),
            pltpu.VMEM((tiles, 1, length), jnp.float32),
            pltpu.VMEM((tiles, CAP, length), jnp.float32),
            pltpu.VMEM((tiles, 1, length), jnp.float32),
            pltpu.VMEM((elements, 2 * length), jnp.float32),
            pltpu.SemaphoreType.DMA,
            pltpu.SemaphoreType.DMA,
            pltpu.SemaphoreType.DMA,
            pltpu.SemaphoreType.DMA((nx,)),
        ],
        compiler_params=pltpu.CompilerParams(
            collective_id=0, has_side_effects=True, vmem_limit_bytes=40 * 1024 * 1024
        ),
        name="exchange",
    )(owner, element, rows)


def local(thermal_rows, row_owner, row_element, modulus, birth, start_disp, bounds):
    depth = modulus.shape[0]
    breadth = modulus.shape[1]
    length = modulus.shape[2]
    elements = depth * breadth
    count = thermal_rows.shape[0]
    summed_rows = exchange(row_owner.reshape(1, count), row_element.reshape(1, count), thermal_rows, elements)
    increment = summed_rows.reshape(depth, breadth, length)
    stress = modulus * increment
    lower = bounds[0]
    upper = bounds[1]
    theta = (upper + lower) / 2.0
    delta = (upper - lower) / 2.0
    sigma = theta / delta
    ratio_now = 1.0 / sigma
    field = start_disp
    step_field = jnp.zeros_like(field)
    stress_ext = with_halo(stress, (("gx", 1), ("gy", 2)), 1)
    load = load_from(jnp.pad(stress_ext, ((1, 1), (0, 0), (0, 0))))
    first_padded = padded_field(field)
    for sweep in range(SWEEPS):
        active = modulus * jnp.where(birth <= sweep, 1.0, SOFTENED).astype(jnp.float32)
        if sweep == 0:
            padded = first_padded
        else:
            padded = padded_field(field)
        residual = load - operate(padded, active)
        scaled = residual / (DIAGONAL_WEIGHT * active)
        step_field, ratio_now = advance(step_field, scaled, sweep, ratio_now, sigma, delta, theta)
        field = field + step_field
    return field


def solution(mesh):
    placed = (
        P(("gx", "gy"), None),
        P(("gx", "gy"), None),
        P(("gx", "gy"), None),
        P(None, "gx", "gy"),
        P(None, "gx", "gy"),
        P(None, None, "gx", "gy"),
        P(),
    )
    return jax.shard_map(
        local, mesh=mesh, in_specs=placed, out_specs=P(None, None, "gx", "gy"), check_vma=False
    )
```

```python
import functools

import jax
import jax.numpy as jnp
from jax import lax
from jax.experimental import pallas as pl
from jax.experimental.pallas import tpu as pltpu
from jax.sharding import PartitionSpec as P

SWEEPS = 4
CAP = 24
NZ = 64
CX = 16
CY = 128
ROWS = 8
PARTS = NZ // ROWS
SLAB = (PARTS, ROWS, CY)
DIAGONAL_WEIGHT = 14.5
COUPLING = 0.25
SOFTENED = 0.05


MESH = pl.DeviceIdType.MESH


def halves(values):
    high = values.astype(jnp.bfloat16)
    low = (values - high.astype(jnp.float32)).astype(jnp.bfloat16)
    return high, low


def onehot(matches):
    return jnp.where(matches, 1.0, 0.0).astype(jnp.bfloat16)


def exchange_kernel(
    nx, ny, owner_ref, element_ref, rows_ref, out_ref,
    split_ref, place_ref, send_rows, send_ids, got_rows, got_ids, total,
    ids_send_sem, ids_recv_sem, rows_send_sem, rows_recv_sem,
):
    tiles = nx * ny
    count = rows_ref.shape[0]
    length = rows_ref.shape[1]
    elements = out_ref.shape[0]
    group = ny * CAP
    gx = lax.axis_index("gx")
    gy = lax.axis_index("gy")

    def there(step):
        return lax.rem(gx + step // ny, nx), lax.rem(gy + lax.rem(step, ny), ny)

    barrier = pltpu.get_barrier_semaphore()

    def greet(step, carry):
        pl.semaphore_signal(barrier, inc=1, device_id=there(step), device_id_type=MESH)
        return carry

    lax.fori_loop(1, tiles, greet, 0)

    owner = owner_ref[...]
    given = element_ref[...]
    depth_index = given // CX
    element = lax.rem(given, CX) * NZ + lax.rem(depth_index, PARTS) * ROWS + depth_index // PARTS + 1
    tile_of = lax.broadcasted_iota(jnp.int32, (tiles, count), 0)
    member = jnp.where(tile_of == owner, 1.0, 0.0)
    member16 = member.astype(jnp.bfloat16)
    block = 256
    earlier = onehot(
        lax.broadcasted_iota(jnp.int32, (block, block), 0) < lax.broadcasted_iota(jnp.int32, (block, block), 1)
    )
    carry = jnp.zeros((tiles, 1), jnp.float32)
    slots = []
    for first in range(0, count, block):
        part = member[:, first : first + block]
        before = jnp.dot(member16[:, first : first + block], earlier, preferred_element_type=jnp.float32) + carry
        slots.append(jnp.sum(before * part, axis=0, keepdims=True))
        carry = carry + jnp.sum(part, axis=1, keepdims=True)
    slot = jnp.concatenate(slots, axis=1).astype(jnp.int32)
    place_ref[...] = owner * CAP + slot

    weighed = jnp.concatenate(
        [
            (member * (element // 32).astype(jnp.float32)).astype(jnp.bfloat16),
            (member * lax.rem(element, 32).astype(jnp.float32)).astype(jnp.bfloat16),
        ],
        axis=0,
    )
    slot_of = onehot(lax.broadcasted_iota(jnp.int32, (length, count), 0) == slot)
    both = lax.dot_general(weighed, slot_of, (((1,), (1,)), ((), ())), preferred_element_type=jnp.float32)
    send_ids[...] = (32.0 * both[:tiles] + both[tiles:]).reshape(tiles, 1, length)

    high, low = halves(rows_ref[...])
    split_ref[:, :length] = high
    split_ref[:, length:] = low

    pl.semaphore_wait(barrier, tiles - 1)

    def number(device):
        return device[0] * ny + device[1]

    def send_id(step, carry):
        to = there(step)
        pltpu.make_async_remote_copy(
            src_ref=send_ids.at[number(to)],
            dst_ref=got_ids.at[step],
            send_sem=ids_send_sem,
            recv_sem=ids_recv_sem,
            device_id=to,
            device_id_type=MESH,
        ).start()
        return carry

    lax.fori_loop(1, tiles, send_id, 0)
    got_ids[0] = send_ids[number((gx, gy))]

    def pack(turn, carry):
        tile_x = lax.rem(gx + turn, nx)
        base = tile_x * group
        wanted = base + lax.broadcasted_iota(jnp.int32, (group, count), 0)
        pick = onehot(wanted == place_ref[...])
        picked = jnp.dot(pick, split_ref[...], preferred_element_type=jnp.float32)
        packed = (picked[:, :length] + picked[:, length:]).reshape(ny, CAP, length)
        send_rows[pl.ds(tile_x * ny, ny)] = packed

        def send(turn_y, carry):
            tile_y = lax.rem(gy + turn_y, ny)
            pltpu.make_async_remote_copy(
                src_ref=send_rows.at[tile_x * ny + tile_y],
                dst_ref=got_rows.at[turn * ny + turn_y],
                send_sem=rows_send_sem,
                recv_sem=rows_recv_sem.at[turn],
                device_id=(tile_x, tile_y),
                device_id_type=MESH,
            ).start()
            return carry

        @pl.when(turn == 0)
        def _():
            lax.fori_loop(1, ny, send, 0)

        @pl.when(turn > 0)
        def _():
            lax.fori_loop(0, ny, send, 0)

        return carry

    lax.fori_loop(0, nx, pack, 0)
    got_rows[0] = send_rows[number((gx, gy))]

    rest = pl.ds(1, tiles - 1)
    pltpu.make_async_copy(got_ids.at[rest], got_ids.at[rest], ids_recv_sem).wait()

    spread = onehot(
        lax.broadcasted_iota(jnp.int32, (length, group), 0)
        == lax.rem(lax.broadcasted_iota(jnp.int32, (length, group), 1), CAP)
    )
    own_lane = lax.broadcasted_iota(jnp.int32, (ny, group), 0) == lax.broadcasted_iota(jnp.int32, (ny, group), 1) // CAP
    total[...] = jnp.zeros_like(total)

    def collect(turn, carry):
        @pl.when(turn == 0)
        def _():
            part = got_rows.at[pl.ds(1, ny - 1)]
            pltpu.make_async_copy(part, part, rows_recv_sem.at[0]).wait()

        @pl.when(turn > 0)
        def _():
            part = got_rows.at[pl.ds(turn * ny, ny)]
            pltpu.make_async_copy(part, part, rows_recv_sem.at[turn]).wait()

        ids = got_ids[pl.ds(turn * ny, ny)].reshape(ny, length)
        ids_high = jnp.floor(ids * (1.0 / 32.0))
        ids_low = ids - 32.0 * ids_high
        wide = 32.0 * jnp.dot(ids_high.astype(jnp.bfloat16), spread, preferred_element_type=jnp.float32) + jnp.dot(
            ids_low.astype(jnp.bfloat16), spread, preferred_element_type=jnp.float32
        )
        flat = jnp.sum(jnp.where(own_lane, wide, 0.0), axis=0, keepdims=True).astype(jnp.int32) - 1
        place = onehot(lax.broadcasted_iota(jnp.int32, (elements, group), 0) == flat)
        high, low = halves(got_rows[pl.ds(turn * ny, ny)].reshape(group, length))
        total[...] += jnp.dot(place, jnp.concatenate([high, low], axis=1), preferred_element_type=jnp.float32)
        return carry

    lax.fori_loop(0, nx, collect, 0)
    out_ref[...] = total[:, :length] + total[:, length:]

    pltpu.make_async_copy(send_ids.at[rest], send_ids.at[rest], ids_send_sem).wait()
    pltpu.make_async_copy(send_rows.at[rest], send_rows.at[rest], rows_send_sem).wait()


def exchange(owner, element, rows, elements):
    nx, ny = lax.axis_size("gx"), lax.axis_size("gy")
    tiles = nx * ny
    count, length = rows.shape
    return pl.pallas_call(
        functools.partial(exchange_kernel, nx, ny),
        out_shape=jax.ShapeDtypeStruct((elements, length), jnp.float32),
        in_specs=[pl.BlockSpec(memory_space=pltpu.VMEM)] * 3,
        out_specs=pl.BlockSpec(memory_space=pltpu.VMEM),
        scratch_shapes=[
            pltpu.VMEM((count, 2 * length), jnp.bfloat16),
            pltpu.VMEM((1, count), jnp.int32),
            pltpu.VMEM((tiles, CAP, length), jnp.float32),
            pltpu.VMEM((tiles, 1, length), jnp.float32),
            pltpu.VMEM((tiles, CAP, length), jnp.float32),
            pltpu.VMEM((tiles, 1, length), jnp.float32),
            pltpu.VMEM((elements, 2 * length), jnp.float32),
            pltpu.SemaphoreType.DMA,
            pltpu.SemaphoreType.DMA,
            pltpu.SemaphoreType.DMA,
            pltpu.SemaphoreType.DMA((nx,)),
        ],
        compiler_params=pltpu.CompilerParams(
            collective_id=0, has_side_effects=True, vmem_limit_bytes=40 * 1024 * 1024
        ),
        name="exchange",
    )(owner, element, rows)


def lanes():
    return lax.broadcasted_iota(jnp.int32, (ROWS, CY), 1)


def up(slab):
    row = lax.broadcasted_iota(jnp.int32, (ROWS, CY), 0)
    first = jnp.where(row == ROWS - 1, 0.0, pltpu.roll(slab[0], ROWS - 1, 0))
    return jnp.concatenate([slab[1:], first[None]], axis=0)


def down(slab):
    row = lax.broadcasted_iota(jnp.int32, (ROWS, CY), 0)
    last = jnp.where(row == 0, 0.0, pltpu.roll(slab[PARTS - 1], 1, 0))
    return jnp.concatenate([last[None], slab[:-1]], axis=0)


def pack_ends(slab, x, packed_ref):
    pair = lax.rem(lanes() + 1, CY) // 2
    ends = slab[0]
    for part in range(1, PARTS):
        ends = jnp.where(pair == part, pltpu.roll(slab[part], 2 * part, 1), ends)
    turn = lax.rem(x, 8)
    ends = pltpu.roll(ends, 2 * PARTS * turn, 1)
    packed_ref[x // 8] = jnp.where(pair // PARTS == turn, ends, packed_ref[x // 8])


def merge_ends(from_left, from_right):
    return jnp.where(lax.rem(lanes(), 2) == 0, pltpu.roll(from_left, 1, 1), pltpu.roll(from_right, CY - 1, 1))


def beside(slab, ends, turn):
    lane = lanes()
    ends = pltpu.roll(ends, lax.rem(CY - 2 * PARTS * turn, CY), 1)
    left, right = [], []
    for part in range(PARTS):
        mine = ends if part == 0 else pltpu.roll(ends, CY - 2 * part, 1)
        left.append(jnp.where(lane == 0, mine, pltpu.roll(slab[part], 1, 1)))
        right.append(jnp.where(lane == CY - 1, mine, pltpu.roll(slab[part], CY - 1, 1)))
    return jnp.stack(left), jnp.stack(right)


def sweep_kernel(
    nx, ny, bounds_ref, increment_ref, modulus_ref, birth_ref, start_ref, out_ref,
    fields, stress, inverse, forces, born, steps, mixed,
    packed, packed_stress, got_ends, got_stress_ends, ends, ends_stress,
    face_send, face_recv, side_send, side_recv, corner_send, corner_recv,
    stress_face_send, stress_face_recv, stress_side_send, stress_side_recv,
):
    gx = lax.axis_index("gx")
    gy = lax.axis_index("gy")
    has = {-1: (gx > 0, gy > 0), 1: (gx < nx - 1, gy < ny - 1)}
    places = [(a, b) for a in (-1, 0, 1) for b in (-1, 0, 1) if (a, b) != (0, 0)]

    def present(a, b):
        if a == 0:
            return has[b][1]
        if b == 0:
            return has[a][0]
        return jnp.logical_and(has[a][0], has[b][1])

    barrier = pltpu.get_barrier_semaphore()
    for a, b in places:

        @pl.when(present(a, b))
        def _(a=a, b=b):
            pl.semaphore_signal(barrier, inc=1, device_id=(gx + a, gy + b), device_id_type=MESH)

    zeros = jnp.zeros((ROWS, CY), jnp.float32)
    for side, slab_at, group_at in ((-1, 0, 0), (1, CX + 1, 3)):

        @pl.when(jnp.logical_not(has[side][0]))
        def _(slab_at=slab_at, group_at=group_at):
            stress[slab_at] = jnp.zeros(SLAB, jnp.float32)
            for sweep in range(SWEEPS):
                for c in range(3):
                    fields[sweep, c, slab_at] = jnp.zeros(SLAB, jnp.float32)
                    for hand in range(2):
                        got_ends[sweep, hand, c, group_at] = zeros

        @pl.when(jnp.logical_not(has[side][1]))
        def _(hand=(side + 1) // 2):
            for group in range(2):
                got_stress_ends[hand, group] = zeros
            for sweep in range(SWEEPS):
                for c in range(3):
                    for group in range(4):
                        got_ends[sweep, hand, c, group] = zeros

    def rows_of(x, part):
        return pl.ds(part * CX + x, ROWS, stride=CX * PARTS)

    def take(ref, x):
        return jnp.stack([ref[rows_of(x, part), :] for part in range(PARTS)])

    def begin(x, carry):
        for c in range(3):
            slab = take(start_ref.at[c], x)
            fields[0, c, x + 1] = slab
            pack_ends(slab, x, packed.at[0, c])
        return carry

    lax.fori_loop(0, CX, begin, 0)

    def strain(x, carry):
        modulus = take(modulus_ref, x)
        inverse[x] = 1.0 / (DIAGONAL_WEIGHT * modulus)
        born[x] = take(birth_ref, x)
        slab = modulus * increment_ref[pl.ds(x * NZ, NZ), :].reshape(SLAB)
        stress[x + 1] = slab
        pack_ends(slab, x, packed_stress)
        return carry

    lax.fori_loop(0, CX, strain, 0)

    columns = 1 + (gx + nx - 1) // nx + (2 * nx - 2 - gx) // nx
    lines = 1 + (gy + ny - 1) // ny + (2 * ny - 2 - gy) // ny
    pl.semaphore_wait(barrier, columns * lines - 1)

    def face(sweep, a):
        mine, theirs = (1, CX + 1) if a < 0 else (CX, 0)
        return pltpu.make_async_remote_copy(
            src_ref=fields.at[sweep, :, mine], dst_ref=fields.at[sweep, :, theirs],
            send_sem=face_send.at[sweep, (a + 1) // 2], recv_sem=face_recv.at[sweep, (1 - a) // 2],
            device_id=(gx + a, gy), device_id_type=MESH,
        )

    def side(sweep, b):
        return pltpu.make_async_remote_copy(
            src_ref=packed.at[sweep], dst_ref=got_ends.at[sweep, (1 - b) // 2, :, pl.ds(1, 2)],
            send_sem=side_send.at[sweep, (b + 1) // 2], recv_sem=side_recv.at[sweep, (1 - b) // 2],
            device_id=(gx, gy + b), device_id_type=MESH,
        )

    def corner(sweep, a, b):
        mine, theirs = (0, 3) if a < 0 else (1, 0)
        return pltpu.make_async_remote_copy(
            src_ref=packed.at[sweep, :, mine], dst_ref=got_ends.at[sweep, (1 - b) // 2, :, theirs],
            send_sem=corner_send.at[sweep, a + 1 + (b + 1) // 2], recv_sem=corner_recv.at[sweep, 1 - a + (1 - b) // 2],
            device_id=(gx + a, gy + b), device_id_type=MESH,
        )

    def stress_face(a):
        mine, theirs = (1, CX + 1) if a < 0 else (CX, 0)
        return pltpu.make_async_remote_copy(
            src_ref=stress.at[mine], dst_ref=stress.at[theirs],
            send_sem=stress_face_send.at[(a + 1) // 2], recv_sem=stress_face_recv.at[(1 - a) // 2],
            device_id=(gx + a, gy), device_id_type=MESH,
        )

    def stress_side(b):
        return pltpu.make_async_remote_copy(
            src_ref=packed_stress, dst_ref=got_stress_ends.at[(1 - b) // 2],
            send_sem=stress_side_send.at[(b + 1) // 2], recv_sem=stress_side_recv.at[(1 - b) // 2],
            device_id=(gx, gy + b), device_id_type=MESH,
        )

    def over(copies, do):
        for where, copy in copies:

            @pl.when(present(*where))
            def _(copy=copy):
                do(copy())

    def faces(sweep):
        return [((a, 0), lambda a=a: face(sweep, a)) for a in (-1, 1)]

    def edges(sweep):
        return [((0, b), lambda b=b: side(sweep, b)) for b in (-1, 1)] + [
            ((a, b), lambda a=a, b=b: corner(sweep, a, b)) for a in (-1, 1) for b in (-1, 1)
        ]

    of_stress = [((a, 0), lambda a=a: stress_face(a)) for a in (-1, 1)] + [
        ((0, b), lambda b=b: stress_side(b)) for b in (-1, 1)
    ]

    def arrival(ref, sem):
        return lambda: pltpu.make_async_copy(ref, ref, sem)

    def from_faces(sweep):
        return [
            ((a, 0), arrival(fields.at[sweep, :, 0 if a < 0 else CX + 1], face_recv.at[sweep, (a + 1) // 2])) for a in (-1, 1)
        ]

    def from_edges(sweep):
        return [
            ((0, b), arrival(got_ends.at[sweep, (b + 1) // 2, :, pl.ds(1, 2)], side_recv.at[sweep, (b + 1) // 2]))
            for b in (-1, 1)
        ] + [
            (
                (a, b),
                arrival(
                    got_ends.at[sweep, (b + 1) // 2, :, 0 if a < 0 else 3],
                    corner_recv.at[sweep, a + 1 + (b + 1) // 2],
                ),
            )
            for a in (-1, 1)
            for b in (-1, 1)
        ]

    of_stress_arrived = [
        ((a, 0), arrival(stress.at[0 if a < 0 else CX + 1], stress_face_recv.at[(a + 1) // 2])) for a in (-1, 1)
    ] + [((0, b), arrival(got_stress_ends.at[(b + 1) // 2], stress_side_recv.at[(b + 1) // 2])) for b in (-1, 1)]

    def start(copy):
        copy.start()

    def receive(copy):
        copy.wait()

    def finish(copy):
        copy.wait_send()

    over(of_stress, start)
    over(edges(0), start)
    over(faces(0), start)

    lower = jnp.full((ROWS, CY), bounds_ref[0], jnp.float32)
    upper = jnp.full((ROWS, CY), bounds_ref[1], jnp.float32)
    theta = (upper + lower) / 2.0
    delta = (upper - lower) / 2.0
    sigma = theta / delta
    ratio = 1.0 / sigma

    over(of_stress_arrived, receive)
    for group in range(2):
        ends_stress[group] = merge_ends(got_stress_ends[0, group], got_stress_ends[1, group])

    def force(x, carry):
        middle = stress[x + 1]
        left, right = beside(middle, ends_stress[x // 8], lax.rem(x, 8))
        scale = 0.5 * inverse[x]
        forces[0, x] = scale * (up(middle) - down(middle))
        forces[1, x] = scale * (stress[x + 2] - stress[x])
        forces[2, x] = scale * (right - left)
        return carry

    lax.fori_loop(0, CX, force, 0)

    for sweep in range(SWEEPS):
        last = sweep == SWEEPS - 1
        over(from_edges(sweep) + from_faces(sweep), receive)
        for c in range(3):
            for group in range(4):
                ends[c, group] = merge_ends(got_ends[sweep, 0, c, group], got_ends[sweep, 1, c, group])

        def along(at, carry, sweep=sweep):
            for c in range(3):
                slab = fields[sweep, c, at]
                left, right = beside(slab, ends[c, (at + 7) // 8], lax.rem(at + 7, 8))
                mixed[c, at] = (left + right) + 2.0 * slab
                mixed[3 + c, at] = right - left
            return carry

        lax.fori_loop(0, CX + 2, along, 0)

        if sweep == 0:
            gain = 1.0 / theta
        else:
            ratio_next = 1.0 / (2.0 * sigma - ratio)
            keep = ratio_next * ratio
            gain = 2.0 * ratio_next / delta
            ratio = ratio_next

        def across(x, sweep=sweep, last=last, gain=gain, keep=None if sweep == 0 else keep):
            at = x + 1
            softer = jnp.where(born[x] <= sweep, 1.0, 1.0 / SOFTENED)
            crossed = (
                (fields[sweep, 1, at + 1] - fields[sweep, 1, at - 1]) + mixed[5, at],
                fields[sweep, 0, at + 1] - fields[sweep, 0, at - 1],
                mixed[3, at],
            )
            for c in range(3):
                around = (mixed[c, at - 1] + mixed[c, at + 1]) + 2.0 * mixed[c, at]
                around = (up(around) + down(around)) + 2.0 * around
                coupled = up(crossed[c]) - down(crossed[c])
                if c == 1:
                    coupled = coupled + (mixed[5, at + 1] - mixed[5, at - 1])
                if c == 2:
                    coupled = coupled + (mixed[4, at + 1] - mixed[4, at - 1])
                around = around + COUPLING * coupled
                slab = fields[sweep, c, at]
                scaled = (
                    (0.25 / DIAGONAL_WEIGHT) * around
                    - ((DIAGONAL_WEIGHT + 2.0) / DIAGONAL_WEIGHT) * slab
                    + softer * forces[c, x]
                )
                step = gain * scaled
                if sweep:
                    step = step + keep * steps[c, x]
                moved = slab + step
                if last:
                    for part in range(PARTS):
                        out_ref[c, rows_of(x, part), :] = moved[part]
                else:
                    steps[c, x] = step
                    fields[sweep + 1, c, at] = moved
                    pack_ends(moved, x, packed.at[sweep + 1, c])

        def across_loop(x, carry, across=across):
            across(x)
            return carry

        if last:
            lax.fori_loop(0, CX, across_loop, 0)
        else:
            lax.fori_loop(0, 2, lambda i, carry, across=across: (across(i * (CX - 1)), carry)[1], 0)
            over(faces(sweep + 1), start)
            lax.fori_loop(1, CX - 1, across_loop, 0)
            over(edges(sweep + 1), start)

    over(of_stress, finish)
    for sweep in range(SWEEPS):
        over(edges(sweep) + faces(sweep), finish)


def sweeps(bounds, increment, modulus, birth, start_disp):
    nx, ny = lax.axis_size("gx"), lax.axis_size("gy")
    cells = NZ * CX
    f32 = jnp.float32
    vmem = pl.BlockSpec(memory_space=pltpu.VMEM)
    dma = pltpu.SemaphoreType.DMA
    moved = pl.pallas_call(
        functools.partial(sweep_kernel, nx, ny),
        out_shape=jax.ShapeDtypeStruct((3, cells, CY), f32),
        in_specs=[pl.BlockSpec(memory_space=pltpu.SMEM)] + [vmem] * 4,
        out_specs=vmem,
        scratch_shapes=[
            pltpu.VMEM((SWEEPS, 3, CX + 2) + SLAB, f32),
            pltpu.VMEM((CX + 2,) + SLAB, f32),
            pltpu.VMEM((CX,) + SLAB, f32),
            pltpu.VMEM((3, CX) + SLAB, f32),
            pltpu.VMEM((CX,) + SLAB, jnp.int32),
            pltpu.VMEM((3, CX) + SLAB, f32),
            pltpu.VMEM((6, CX + 2) + SLAB, f32),
            pltpu.VMEM((SWEEPS, 3, 2, ROWS, CY), f32),
            pltpu.VMEM((2, ROWS, CY), f32),
            pltpu.VMEM((SWEEPS, 2, 3, 4, ROWS, CY), f32),
            pltpu.VMEM((2, 2, ROWS, CY), f32),
            pltpu.VMEM((3, 4, ROWS, CY), f32),
            pltpu.VMEM((2, ROWS, CY), f32),
            dma((SWEEPS, 2)), dma((SWEEPS, 2)), dma((SWEEPS, 2)), dma((SWEEPS, 2)), dma((SWEEPS, 4)), dma((SWEEPS, 4)),
            dma((2,)), dma((2,)), dma((2,)), dma((2,)),
        ],
        compiler_params=pltpu.CompilerParams(
            collective_id=1, has_side_effects=True, vmem_limit_bytes=40 * 1024 * 1024
        ),
        name="sweeps",
    )(
        bounds, increment, modulus.reshape(cells, CY), birth.reshape(cells, CY), start_disp.reshape(3, cells, CY)
    )
    return moved.reshape(start_disp.shape)


def local(thermal_rows, row_owner, row_element, modulus, birth, start_disp, bounds):
    count = thermal_rows.shape[0]
    increment = exchange(row_owner.reshape(1, count), row_element.reshape(1, count), thermal_rows, NZ * CX)
    return sweeps(bounds, increment, modulus, birth, start_disp)


def solution(mesh):
    placed = (
        P(("gx", "gy"), None),
        P(("gx", "gy"), None),
        P(("gx", "gy"), None),
        P(None, "gx", "gy"),
        P(None, "gx", "gy"),
        P(None, None, "gx", "gy"),
        P(),
    )
    return jax.shard_map(
        local, mesh=mesh, in_specs=placed, out_specs=P(None, None, "gx", "gy"), check_vma=False
    )
```

```python
import functools

import jax
import jax.numpy as jnp
from jax import lax
from jax.experimental import pallas as pl
from jax.experimental.pallas import tpu as pltpu
from jax.sharding import PartitionSpec as P

SWEEPS = 4
CAP = 24
NZ = 64
CX = 16
CY = 128
ROWS = 8
PARTS = 8
HALF = CY // 2
CELLS = NZ * CX
SLABS = CX + 2
SLAB = (PARTS, ROWS, CY)
DIAGONAL_WEIGHT = 14.5
COUPLING = 0.25
SOFTENED = 0.05

MESH = pl.DeviceIdType.MESH
F32 = jnp.float32
BF16 = jnp.bfloat16


def halves(values):
    high = values.astype(BF16)
    low = (values - high.astype(F32)).astype(BF16)
    return high, low


def onehot(matches):
    return jnp.where(matches, 1.0, 0.0).astype(BF16)


def iota(shape, dim):
    return lax.broadcasted_iota(jnp.int32, shape, dim)


def product(left, right):
    return jnp.dot(left, right, preferred_element_type=F32)


def row_index():
    return iota((ROWS, CY), 0)


def in_first_half():
    return iota((ROWS, CY), 1) < HALF


def up(slab, ends):
    first = pltpu.roll(slab[0], ROWS - 1, 0)
    turned = jnp.where(in_first_half(), pltpu.roll(first, HALF, 1), ends)
    return jnp.concatenate([slab[1:], jnp.where(row_index() == ROWS - 1, turned, first)[None]], axis=0)


def down(slab, ends):
    last = pltpu.roll(slab[PARTS - 1], 1, 0)
    turned = jnp.where(in_first_half(), ends, pltpu.roll(last, HALF, 1))
    return jnp.concatenate([jnp.where(row_index() == 0, turned, last)[None], slab[:-1]], axis=0)


def end_row(slab):
    return jnp.where(iota((1, CY), 1) < HALF, slab[0][:1], pltpu.roll(slab[PARTS - 1], 1, 0)[:1])


def turn_halves(values):
    return pltpu.roll(values, HALF, 1)


def kernel(
    nx, ny,
    owner_hbm, element_hbm, rows_hbm, modulus_hbm, birth_hbm, start_hbm, bounds_ref,
    out_ref,
    owner_ref, element_ref, rows_ref, modulus_ref, birth_ref, start_ref, in_sem,
    split_ref, place_ref, send_rows, send_ids, got_rows, got_ids, total,
    ids_send_sem, ids_recv_sem, rows_send_sem, rows_recv_sem,
    fields, stress, inverse, forces, born, steps, summed, differed, sliced,
    along_matrix, turning,
    packed, packed_stress, got_ends, got_stress_ends, ends, ends_summed, ends_differed, ends_added,
    face_send, face_recv, side_send, side_recv, corner_send, corner_recv,
    stress_face_send, stress_face_recv, stress_side_send, stress_side_recv,
):
    tiles = nx * ny
    count = rows_ref.shape[0]
    group = ny * CAP
    gx = lax.axis_index("gx")
    gy = lax.axis_index("gy")

    loads = [
        pltpu.make_async_copy(source, target, in_sem.at[i])
        for i, (source, target) in enumerate(
            [
                (owner_hbm, owner_ref), (element_hbm, element_ref), (rows_hbm, rows_ref),
                (start_hbm, start_ref), (modulus_hbm, modulus_ref), (birth_hbm, birth_ref),
            ]
        )
    ]
    for load in loads:
        load.start()

    def there(step):
        return lax.rem(gx + step // ny, nx), lax.rem(gy + lax.rem(step, ny), ny)

    def number(device):
        return device[0] * ny + device[1]

    barrier = pltpu.get_barrier_semaphore()

    def greet(step, carry):
        pl.semaphore_signal(barrier, inc=1, device_id=there(step), device_id_type=MESH)
        return carry

    lax.fori_loop(1, tiles, greet, 0)

    has = {-1: (gx > 0, gy > 0), 1: (gx < nx - 1, gy < ny - 1)}

    def present(a, b):
        if a == 0:
            return has[b][1]
        if b == 0:
            return has[a][0]
        return jnp.logical_and(has[a][0], has[b][1])

    def over(copies, do):
        for where, copy in copies:

            @pl.when(present(*where))
            def _(copy=copy):
                do(copy())

    loads[0].wait()
    loads[1].wait()
    owner = owner_ref[...]
    given = element_ref[...]
    depth_index = given // CX
    element = lax.rem(given, CX) * NZ + depth_index + 1
    member = jnp.where(iota((tiles, count), 0) == owner, 1.0, 0.0)
    member16 = member.astype(BF16)
    block = 256
    earlier = onehot(iota((block, block), 0) < iota((block, block), 1))
    carried = jnp.zeros((tiles, 1), F32)
    slots = []
    for first in range(0, count, block):
        part = member[:, first : first + block]
        before = product(member16[:, first : first + block], earlier) + carried
        slots.append(jnp.sum(before * part, axis=0, keepdims=True))
        carried = carried + jnp.sum(part, axis=1, keepdims=True)
    slot = jnp.concatenate(slots, axis=1).astype(jnp.int32)
    place_ref[...] = owner * CAP + slot

    weighed = jnp.concatenate(
        [
            (member * (element // 32).astype(F32)).astype(BF16),
            (member * lax.rem(element, 32).astype(F32)).astype(BF16),
        ],
        axis=0,
    )
    slot_of = onehot(iota((CY, count), 0) == slot)
    both = lax.dot_general(weighed, slot_of, (((1,), (1,)), ((), ())), preferred_element_type=F32)
    send_ids[...] = (32.0 * both[:tiles] + both[tiles:]).reshape(tiles, 1, CY)

    loads[2].wait()
    high, low = halves(rows_ref[...])
    split_ref[:, :CY] = high
    split_ref[:, CY:] = low

    pl.semaphore_wait(barrier, tiles - 1)

    def send_id(step, carry):
        to = there(step)
        pltpu.make_async_remote_copy(
            src_ref=send_ids.at[number(to)], dst_ref=got_ids.at[step],
            send_sem=ids_send_sem, recv_sem=ids_recv_sem,
            device_id=to, device_id_type=MESH,
        ).start()
        return carry

    lax.fori_loop(1, tiles, send_id, 0)
    got_ids[0] = send_ids[number((gx, gy))]

    def pack_rows(turn, carry):
        tile_x = lax.rem(gx + turn, nx)
        wanted = tile_x * group + iota((group, count), 0)
        picked = product(onehot(wanted == place_ref[...]), split_ref[...])
        send_rows[pl.ds(tile_x * ny, ny)] = (picked[:, :CY] + picked[:, CY:]).reshape(ny, CAP, CY)

        def send(turn_y, carry):
            tile_y = lax.rem(gy + turn_y, ny)
            pltpu.make_async_remote_copy(
                src_ref=send_rows.at[tile_x * ny + tile_y], dst_ref=got_rows.at[turn * ny + turn_y],
                send_sem=rows_send_sem, recv_sem=rows_recv_sem.at[turn],
                device_id=(tile_x, tile_y), device_id_type=MESH,
            ).start()
            return carry

        @pl.when(turn == 0)
        def _():
            lax.fori_loop(1, ny, send, 0)

        @pl.when(turn > 0)
        def _():
            lax.fori_loop(0, ny, send, 0)

        return carry

    lax.fori_loop(0, nx, pack_rows, 0)
    got_rows[0] = send_rows[number((gx, gy))]

    zeros = jnp.zeros((ROWS, CY), F32)
    for hand, slab_at, group_at in ((-1, 0, 0), (1, CX + 1, 3)):

        @pl.when(jnp.logical_not(has[hand][0]))
        def _(slab_at=slab_at, group_at=group_at):
            stress[slab_at] = jnp.zeros(SLAB, F32)
            for sweep in range(SWEEPS):
                for c in range(3):
                    fields[sweep, c, slab_at] = jnp.zeros(SLAB, F32)
                    for side_at in range(2):
                        got_ends[sweep, side_at, c, group_at] = zeros

        @pl.when(jnp.logical_not(has[hand][1]))
        def _(side_at=(hand + 1) // 2):
            got_stress_ends[side_at] = jnp.zeros((2, ROWS, CY), F32)
            for sweep in range(SWEEPS):
                for c in range(3):
                    got_ends[sweep, side_at, c] = jnp.zeros((4, ROWS, CY), F32)

    row, column = iota((2 * CY, 2 * CY), 0), iota((2 * CY, 2 * CY), 1)
    k, z = lax.rem(row, CY), lax.rem(column, CY)
    off = jnp.where(k // NZ == z // NZ, k - z, 2)
    after, before = jnp.where(off == 1, 1.0, 0.0), jnp.where(off == -1, 1.0, 0.0)
    sums = jnp.where(off == 0, 2.0, after + before)
    along_matrix[...] = jnp.where(column < CY, sums, after - before).astype(BF16)

    first_half = iota((2 * NZ // 2, CY), 1) < HALF

    def slabs_of(pair, at):
        turned = pair.T
        begin, end = turned[:NZ], turned[NZ:]
        slabs = []
        for odd, values in enumerate(
            (jnp.where(first_half, begin, turn_halves(end)), jnp.where(first_half, turn_halves(begin), end))
        ):
            turning[2 * at + odd] = values
            slabs.append(jnp.stack([turning[2 * at + odd, pl.ds(part, ROWS, stride=PARTS), :] for part in range(PARTS)]))
        return slabs

    def pair_of_slabs(slabs, at):
        for odd in range(2):
            for part in range(PARTS):
                turning[2 * at + odd, pl.ds(part, ROWS, stride=PARTS), :] = slabs[odd][part]
        even, odd = turning[2 * at], turning[2 * at + 1]
        return jnp.concatenate(
            [jnp.where(first_half, even, turn_halves(odd)), jnp.where(first_half, turn_halves(even), odd)], axis=0
        ).T

    def rows_of(x, part):
        return pl.ds(part * ROWS * CX + x, ROWS, stride=CX)

    def take(ref, i):
        return jnp.concatenate([ref[rows_of(2 * i + odd, part), :] for odd in range(2) for part in range(NZ // ROWS)], axis=0)

    def slice_up(slab, at):
        high, low = halves(slab.reshape(NZ, CY))
        sliced[at, :, :CY] = high
        sliced[at, :, CY:] = low

    def merge_ends(from_left, from_right):
        return turn_halves(jnp.where(in_first_half(), from_right, from_left))

    def face(sweep, a):
        mine, theirs = (1, CX + 1) if a < 0 else (CX, 0)
        return pltpu.make_async_remote_copy(
            src_ref=fields.at[sweep, :, mine], dst_ref=fields.at[sweep, :, theirs],
            send_sem=face_send.at[sweep, (a + 1) // 2], recv_sem=face_recv.at[sweep, (1 - a) // 2],
            device_id=(gx + a, gy), device_id_type=MESH,
        )

    def side(sweep, b):
        return pltpu.make_async_remote_copy(
            src_ref=packed.at[sweep], dst_ref=got_ends.at[sweep, (1 - b) // 2, :, pl.ds(1, 2)],
            send_sem=side_send.at[sweep, (b + 1) // 2], recv_sem=side_recv.at[sweep, (1 - b) // 2],
            device_id=(gx, gy + b), device_id_type=MESH,
        )

    def corner(sweep, a, b):
        mine, theirs = (0, 3) if a < 0 else (1, 0)
        return pltpu.make_async_remote_copy(
            src_ref=packed.at[sweep, :, mine], dst_ref=got_ends.at[sweep, (1 - b) // 2, :, theirs],
            send_sem=corner_send.at[sweep, a + 1 + (b + 1) // 2], recv_sem=corner_recv.at[sweep, 1 - a + (1 - b) // 2],
            device_id=(gx + a, gy + b), device_id_type=MESH,
        )

    def stress_face(a):
        mine, theirs = (1, CX + 1) if a < 0 else (CX, 0)
        return pltpu.make_async_remote_copy(
            src_ref=stress.at[mine], dst_ref=stress.at[theirs],
            send_sem=stress_face_send.at[(a + 1) // 2], recv_sem=stress_face_recv.at[(1 - a) // 2],
            device_id=(gx + a, gy), device_id_type=MESH,
        )

    def stress_side(b):
        return pltpu.make_async_remote_copy(
            src_ref=packed_stress, dst_ref=got_stress_ends.at[(1 - b) // 2],
            send_sem=stress_side_send.at[(b + 1) // 2], recv_sem=stress_side_recv.at[(1 - b) // 2],
            device_id=(gx, gy + b), device_id_type=MESH,
        )

    pair_of = (-1, 1)

    def faces(sweep):
        return [((a, 0), lambda a=a: face(sweep, a)) for a in pair_of]

    def edges(sweep):
        return [((0, b), lambda b=b: side(sweep, b)) for b in pair_of] + [
            ((a, b), lambda a=a, b=b: corner(sweep, a, b)) for a in pair_of for b in pair_of
        ]

    stress_faces = [((a, 0), lambda a=a: stress_face(a)) for a in pair_of]
    stress_sides = [((0, b), lambda b=b: stress_side(b)) for b in pair_of]

    def arrival(ref, sem):
        return lambda: pltpu.make_async_copy(ref, ref, sem)

    def from_faces(sweep):
        return [
            ((a, 0), arrival(fields.at[sweep, :, 0 if a < 0 else CX + 1], face_recv.at[sweep, (a + 1) // 2]))
            for a in pair_of
        ]

    def from_edges(sweep):
        return [
            ((0, b), arrival(got_ends.at[sweep, (b + 1) // 2, :, pl.ds(1, 2)], side_recv.at[sweep, (b + 1) // 2]))
            for b in pair_of
        ] + [
            (
                (a, b),
                arrival(
                    got_ends.at[sweep, (b + 1) // 2, :, 0 if a < 0 else 3],
                    corner_recv.at[sweep, a + 1 + (b + 1) // 2],
                ),
            )
            for a in pair_of
            for b in pair_of
        ]

    from_stress_faces = [
        ((a, 0), arrival(stress.at[0 if a < 0 else CX + 1], stress_face_recv.at[(a + 1) // 2])) for a in pair_of
    ]
    from_stress_sides = [
        ((0, b), arrival(got_stress_ends.at[(b + 1) // 2], stress_side_recv.at[(b + 1) // 2])) for b in pair_of
    ]

    def start(copy):
        copy.start()

    def receive(copy):
        copy.wait()

    def finish(copy):
        copy.wait_send()

    def along_own(sweep):
        for c in range(3):
            at = pl.ds(c * SLABS + 1, CX)
            both = product(sliced[at].reshape(CX * NZ, 2 * CY), along_matrix[...])
            summed[at] = both[:, :CY].reshape((CX,) + SLAB)
            differed[at] = both[:, CY:].reshape((CX,) + SLAB)

    def along_halo(sweep):
        over(from_edges(sweep) + from_faces(sweep), receive)
        for c in range(3):
            for g in range(4):
                at = pl.ds(g * ROWS, ROWS)
                ends[c, at] = merge_ends(got_ends[sweep, 0, c, g], got_ends[sweep, 1, c, g])
        halo = [fields[sweep, c, at].reshape(NZ, CY) for c in range(3) for at in (0, CX + 1)]
        high, low = halves(jnp.concatenate(halo + [ends[c] for c in range(3)], axis=0))
        both = product(jnp.concatenate([high, low], axis=1), along_matrix[...])
        for c in range(3):
            for hand, at in enumerate((0, CX + 1)):
                first = (2 * c + hand) * NZ
                summed[c * SLABS + at] = both[first : first + NZ, :CY].reshape(SLAB)
                differed[c * SLABS + at] = both[first : first + NZ, CY:].reshape(SLAB)
            first = 6 * NZ + c * 4 * ROWS
            ends_summed[c] = both[first : first + 4 * ROWS, :CY]
            ends_differed[c] = both[first : first + 4 * ROWS, CY:]

        def near(ref, c, step):
            return ref[c, pl.ds(ROWS + step, CX), :]

        for c in range(3):
            around = (near(ends_summed, c, -1) + near(ends_summed, c, 1)) + 2.0 * near(ends_summed, c, 0)
            if c == 0:
                across = near(ends_differed, 2, 0)
            elif c == 1:
                across = near(ends, 2, 1) - near(ends, 2, -1)
            else:
                across = near(ends_differed, 0, 0) + (near(ends, 1, 1) - near(ends, 1, -1))
            sign = jnp.where(iota((CX, CY), 1) < HALF, -COUPLING, COUPLING)
            ends_added[c] = around + sign * across

    def rest(sweep, x, c):
        at = x + 1

        def field(component, to):
            return fields[sweep, component, to]

        def along_sum(to):
            return summed[c * SLABS + to]

        def along_difference(component, to):
            return differed[component * SLABS + to]

        around = (along_sum(at - 1) + along_sum(at + 1)) + 2.0 * along_sum(at)
        if c == 0:
            across = along_difference(2, at)
        elif c == 1:
            across = field(2, at + 1) - field(2, at - 1)
        else:
            across = along_difference(0, at) + (field(1, at + 1) - field(1, at - 1))
        across = COUPLING * across
        added = ends_added[c, pl.ds(x, 1), :]
        total_around = (up(around + across, added) + down(around - across, added)) + 2.0 * around
        if c < 2:
            total_around = total_around + COUPLING * (along_difference(1 - c, at + 1) - along_difference(1 - c, at - 1))
        return (0.25 / DIAGONAL_WEIGHT) * total_around - ((DIAGONAL_WEIGHT + 2.0) / DIAGONAL_WEIGHT) * field(c, at)

    loads[3].wait()

    def store_ends(slab, x, ref):
        ref[x // ROWS, pl.ds(lax.rem(x, ROWS), 1), :] = end_row(slab)

    def begin(i, carry):
        for c in range(3):
            for odd, slab in enumerate(slabs_of(take(start_ref.at[c], i), c)):
                x = 2 * i + odd
                fields[0, c, x + 1] = slab
                slice_up(slab, c * SLABS + x + 1)
                store_ends(slab, x, packed.at[0, c])
        return carry

    lax.fori_loop(0, CX // 2, begin, 0)
    over(faces(0), start)
    over(edges(0), start)

    loads[4].wait()
    loads[5].wait()

    def material(i, carry):
        for odd, modulus in enumerate(slabs_of(take(modulus_ref, i), 0)):
            x = 2 * i + odd
            stress[x + 1] = modulus
            inverse[x] = 1.0 / (DIAGONAL_WEIGHT * modulus)
        for odd, birth in enumerate(slabs_of(take(birth_ref, i).astype(F32), 1)):
            born[2 * i + odd] = birth
        return carry

    lax.fori_loop(0, CX // 2, material, 0)
    along_own(0)

    lower = jnp.full((ROWS, CY), bounds_ref[0], F32)
    upper = jnp.full((ROWS, CY), bounds_ref[1], F32)
    theta = (upper + lower) / 2.0
    delta = (upper - lower) / 2.0
    sigma = theta / delta
    ratio = 1.0 / sigma

    along_halo(0)

    def first_rest(x, carry):
        for c in range(3):
            steps[c, x] = rest(0, x, c)
        return carry

    lax.fori_loop(0, CX, first_rest, 0, unroll=2)

    others = pl.ds(1, tiles - 1)
    pltpu.make_async_copy(got_ids.at[others], got_ids.at[others], ids_recv_sem).wait()
    spread = onehot(iota((CY, group), 0) == lax.rem(iota((CY, group), 1), CAP))
    own_lane = iota((ny, group), 0) == iota((ny, group), 1) // CAP
    total[...] = jnp.zeros_like(total)

    def collect(turn, carry):
        @pl.when(turn == 0)
        def _():
            part = got_rows.at[pl.ds(1, ny - 1)]
            pltpu.make_async_copy(part, part, rows_recv_sem.at[0]).wait()

        @pl.when(turn > 0)
        def _():
            part = got_rows.at[pl.ds(turn * ny, ny)]
            pltpu.make_async_copy(part, part, rows_recv_sem.at[turn]).wait()

        ids = got_ids[pl.ds(turn * ny, ny)].reshape(ny, CY)
        ids_high = jnp.floor(ids * (1.0 / 32.0))
        ids_low = ids - 32.0 * ids_high
        wide = 32.0 * product(ids_high.astype(BF16), spread) + product(ids_low.astype(BF16), spread)
        flat = jnp.sum(jnp.where(own_lane, wide, 0.0), axis=0, keepdims=True).astype(jnp.int32) - 1
        place = onehot(iota((CELLS, group), 0) == flat)
        high, low = halves(got_rows[pl.ds(turn * ny, ny)].reshape(group, CY))
        total[...] += product(place, jnp.concatenate([high, low], axis=1))
        return carry

    lax.fori_loop(0, nx, collect, 0)

    def strain(i, carry):
        at = pl.ds(2 * i * NZ, 2 * NZ)
        for odd, slab in enumerate(slabs_of(total[at, :CY] + total[at, CY:], 0)):
            x = 2 * i + odd
            slab = stress[x + 1] * slab
            stress[x + 1] = slab
            slice_up(slab, x + 1)
            store_ends(slab, x, packed_stress)
        return carry

    lax.fori_loop(0, CX // 2, strain, 0)
    over(stress_faces, start)
    over(stress_sides, start)
    at = pl.ds(1, CX)
    differed[at] = product(sliced[at].reshape(CX * NZ, 2 * CY), along_matrix[:, CY:]).reshape((CX,) + SLAB)
    over(from_stress_sides, receive)
    for g in range(2):
        ends[0, pl.ds(g * ROWS, ROWS)] = merge_ends(got_stress_ends[0, g], got_stress_ends[1, g])
    over(from_stress_faces, receive)

    def keep_moved(sweep, x, c, moved, step):
        at = x + 1
        steps[c, x] = step
        fields[sweep + 1, c, at] = moved
        slice_up(moved, c * SLABS + at)
        store_ends(moved, x, packed.at[sweep + 1, c])

    def softer(sweep, x):
        return jnp.where(born[x] <= sweep, 1.0, 1.0 / SOFTENED)

    first_gain = 1.0 / theta

    def first_move(x):
        middle = stress[x + 1]
        scale = 0.5 * inverse[x]
        soft = softer(0, x)
        added = ends[0, pl.ds(x, 1), :]
        gradients = (differed[x + 1], stress[x + 2] - stress[x], up(middle, added) - down(middle, added))
        for c, gradient in enumerate(gradients):
            force = scale * gradient
            forces[c, x] = force
            step = first_gain * (steps[c, x] + soft * force)
            keep_moved(0, x, c, fields[0, c, x + 1] + step, step)

    def ends_first(move, sweep):
        lax.fori_loop(0, 2, lambda i, carry: (move(i * (CX - 1)), carry)[1], 0, unroll=2)
        over(faces(sweep + 1), start)
        lax.fori_loop(1, CX - 1, lambda x, carry: (move(x), carry)[1], 0, unroll=2)
        over(edges(sweep + 1), start)
        along_own(sweep + 1)

    ends_first(first_move, 0)

    for sweep in range(1, SWEEPS):
        ratio_next = 1.0 / (2.0 * sigma - ratio)
        keep = ratio_next * ratio
        gain = 2.0 * ratio_next / delta
        ratio = ratio_next
        along_halo(sweep)

        def moves(x, sweep=sweep, keep=keep, gain=gain):
            soft = softer(sweep, x)
            for c in range(3):
                step = gain * (rest(sweep, x, c) + soft * forces[c, x]) + keep * steps[c, x]
                yield c, fields[sweep, c, x + 1] + step, step

        if sweep < SWEEPS - 1:

            def move(x, sweep=sweep, moves=moves):
                for c, moved, step in moves(x):
                    keep_moved(sweep, x, c, moved, step)

            ends_first(move, sweep)
        else:

            def last(i, carry, moves=moves):
                both = [[moved for _, moved, _ in moves(2 * i + odd)] for odd in range(2)]
                for c in range(3):
                    block = pair_of_slabs([both[0][c], both[1][c]], c)
                    for odd in range(2):
                        for part in range(NZ // ROWS):
                            first = odd * NZ + part * ROWS
                            out_ref[c, rows_of(2 * i + odd, part), :] = block[first : first + ROWS]
                return carry

            lax.fori_loop(0, CX // 2, last, 0)

    pltpu.make_async_copy(send_ids.at[others], send_ids.at[others], ids_send_sem).wait()
    pltpu.make_async_copy(send_rows.at[others], send_rows.at[others], rows_send_sem).wait()
    over(stress_faces + stress_sides, finish)
    for sweep in range(SWEEPS):
        over(edges(sweep) + faces(sweep), finish)


def local(thermal_rows, row_owner, row_element, modulus, birth, start_disp, bounds):
    nx, ny = lax.axis_size("gx"), lax.axis_size("gy")
    tiles = nx * ny
    count = thermal_rows.shape[0]
    vmem, dma = pltpu.VMEM, pltpu.SemaphoreType.DMA
    moved = pl.pallas_call(
        functools.partial(kernel, nx, ny),
        out_shape=jax.ShapeDtypeStruct((3, CELLS, CY), F32),
        in_specs=[pl.BlockSpec(memory_space=pl.ANY)] * 6 + [pl.BlockSpec(memory_space=pltpu.SMEM)],
        out_specs=pl.BlockSpec(memory_space=pltpu.VMEM),
        scratch_shapes=[
            vmem((1, count), jnp.int32),
            vmem((1, count), jnp.int32),
            vmem((count, CY), F32),
            vmem((CELLS, CY), F32),
            vmem((CELLS, CY), jnp.int32),
            vmem((3, CELLS, CY), F32),
            dma((6,)),
            vmem((count, 2 * CY), BF16),
            vmem((1, count), jnp.int32),
            vmem((tiles, CAP, CY), F32),
            vmem((tiles, 1, CY), F32),
            vmem((tiles, CAP, CY), F32),
            vmem((tiles, 1, CY), F32),
            vmem((CELLS, 2 * CY), F32),
            dma, dma, dma, dma((nx,)),
            vmem((SWEEPS, 3, SLABS) + SLAB, F32),
            vmem((SLABS,) + SLAB, F32),
            vmem((CX,) + SLAB, F32),
            vmem((3, CX) + SLAB, F32),
            vmem((CX,) + SLAB, F32),
            vmem((3, CX) + SLAB, F32),
            vmem((3 * SLABS,) + SLAB, F32),
            vmem((3 * SLABS,) + SLAB, F32),
            vmem((3 * SLABS, NZ, 2 * CY), BF16),
            vmem((2 * CY, 2 * CY), BF16),
            vmem((6, NZ, CY), F32),
            vmem((SWEEPS, 3, 2, ROWS, CY), F32),
            vmem((2, ROWS, CY), F32),
            vmem((SWEEPS, 2, 3, 4, ROWS, CY), F32),
            vmem((2, 2, ROWS, CY), F32),
            vmem((3, 4 * ROWS, CY), F32),
            vmem((3, 4 * ROWS, CY), F32),
            vmem((3, 4 * ROWS, CY), F32),
            vmem((3, CX, CY), F32),
            dma((SWEEPS, 2)), dma((SWEEPS, 2)), dma((SWEEPS, 2)), dma((SWEEPS, 2)), dma((SWEEPS, 4)), dma((SWEEPS, 4)),
            dma((2,)), dma((2,)), dma((2,)), dma((2,)),
        ],
        compiler_params=pltpu.CompilerParams(
            collective_id=0, has_side_effects=True, vmem_limit_bytes=48 * 1024 * 1024
        ),
        name="weld",
    )(
        row_owner.reshape(1, count), row_element.reshape(1, count), thermal_rows,
        modulus.reshape(CELLS, CY), birth.reshape(CELLS, CY), start_disp.reshape(3, CELLS, CY), bounds,
    )
    return moved.reshape(start_disp.shape)


def solution(mesh):
    placed = (
        P(("gx", "gy"), None),
        P(("gx", "gy"), None),
        P(("gx", "gy"), None),
        P(None, "gx", "gy"),
        P(None, "gx", "gy"),
        P(None, None, "gx", "gy"),
        P(),
    )
    return jax.shard_map(
        local, mesh=mesh, in_specs=placed, out_specs=P(None, None, "gx", "gy"), check_vma=False
    )
```

```python
import functools

import jax
import jax.numpy as jnp
from jax import lax
from jax.experimental import pallas as pl
from jax.experimental.pallas import tpu as pltpu
from jax.sharding import PartitionSpec as P

SWEEPS = 4
CAP = 24
NZ = 64
CX = 16
CY = 128
ROWS = 8
PARTS = 8
HALF = CY // 2
CELLS = NZ * CX
SLABS = CX + 2
SLAB = (PARTS, ROWS, CY)
DIAGONAL_WEIGHT = 14.5
COUPLING = 0.25
SOFTENED = 0.05

MESH = pl.DeviceIdType.MESH
F32 = jnp.float32
BF16 = jnp.bfloat16


def halves(values):
    high = values.astype(BF16)
    low = (values - high.astype(F32)).astype(BF16)
    return high, low


def onehot(matches):
    return jnp.where(matches, 1.0, 0.0).astype(BF16)


def iota(shape, dim):
    return lax.broadcasted_iota(jnp.int32, shape, dim)


def product(left, right):
    return jnp.dot(left, right, preferred_element_type=F32)


def row_index():
    return iota((ROWS, CY), 0)


def in_first_half():
    return iota((ROWS, CY), 1) < HALF


def up(slab, ends):
    first = pltpu.roll(slab[0], ROWS - 1, 0)
    turned = jnp.where(in_first_half(), pltpu.roll(first, HALF, 1), ends)
    return jnp.concatenate([slab[1:], jnp.where(row_index() == ROWS - 1, turned, first)[None]], axis=0)


def down(slab, ends):
    last = pltpu.roll(slab[PARTS - 1], 1, 0)
    turned = jnp.where(in_first_half(), ends, pltpu.roll(last, HALF, 1))
    return jnp.concatenate([jnp.where(row_index() == 0, turned, last)[None], slab[:-1]], axis=0)


def end_row(slab):
    return jnp.where(iota((1, CY), 1) < HALF, slab[0][:1], pltpu.roll(slab[PARTS - 1], 1, 0)[:1])


def turn_halves(values):
    return pltpu.roll(values, HALF, 1)


def kernel(
    nx, ny,
    owner_hbm, element_hbm, rows_hbm, modulus_hbm, birth_hbm, start_hbm, bounds_ref,
    out_ref,
    owner_ref, element_ref, rows_ref, modulus_ref, birth_ref, start_ref, in_sem,
    split_ref, place_ref, send_rows, send_ids, column_ids, got_rows, got_ids, total,
    ready_sem, column_send_sem, column_recv_sem, ids_send_sem, ids_recv_sem, rows_send_sem, rows_recv_sem,
    fields, stress, inverse, forces, born, steps, summed, differed, sliced,
    along_matrix, turning,
    packed, packed_stress, got_ends, got_stress_ends, ends, ends_summed, ends_differed, ends_added,
    face_send, face_recv, side_send, side_recv, corner_send, corner_recv,
    stress_face_send, stress_face_recv, stress_side_send, stress_side_recv,
):
    tiles = nx * ny
    count = rows_ref.shape[0]
    group = ny * CAP
    gx = lax.axis_index("gx")
    gy = lax.axis_index("gy")

    loads = [
        pltpu.make_async_copy(source, target, in_sem.at[i])
        for i, (source, target) in enumerate(
            [
                (owner_hbm, owner_ref), (element_hbm, element_ref), (rows_hbm, rows_ref),
                (start_hbm, start_ref), (modulus_hbm, modulus_ref), (birth_hbm, birth_ref),
            ]
        )
    ]
    for load in loads:
        load.start()

    def in_column(turn):
        return lax.rem(gx + turn, nx), gy

    def in_line(turn):
        return gx, lax.rem(gy + turn, ny)

    barrier = pltpu.get_barrier_semaphore()

    def greet_line(turn, carry):
        pl.semaphore_signal(barrier, inc=1, device_id=in_line(turn), device_id_type=MESH)
        return carry

    def greet_column(turn, carry):
        pl.semaphore_signal(barrier, inc=1, device_id=in_column(turn), device_id_type=MESH)
        return carry

    def tell_column(turn, carry):
        pl.semaphore_signal(ready_sem, inc=1, device_id=in_column(turn), device_id_type=MESH)
        return carry

    lax.fori_loop(1, ny, greet_line, 0)
    lax.fori_loop(1, nx, greet_column, 0)

    has = {-1: (gx > 0, gy > 0), 1: (gx < nx - 1, gy < ny - 1)}

    def present(a, b):
        if a == 0:
            return has[b][1]
        if b == 0:
            return has[a][0]
        return jnp.logical_and(has[a][0], has[b][1])

    def over(copies, do):
        for where, copy in copies:

            @pl.when(present(*where))
            def _(copy=copy):
                do(copy())

    loads[0].wait()
    loads[1].wait()
    owner = owner_ref[...]
    given = element_ref[...]
    depth_index = given // CX
    element = lax.rem(given, CX) * NZ + depth_index + 1
    member = jnp.where(iota((tiles, count), 0) == owner, 1.0, 0.0)
    member16 = member.astype(BF16)
    block = 256
    earlier = onehot(iota((block, block), 0) < iota((block, block), 1))
    carried = jnp.zeros((tiles, 1), F32)
    slots = []
    for first in range(0, count, block):
        part = member[:, first : first + block]
        before = product(member16[:, first : first + block], earlier) + carried
        slots.append(jnp.sum(before * part, axis=0, keepdims=True))
        carried = carried + jnp.sum(part, axis=1, keepdims=True)
    slot = jnp.concatenate(slots, axis=1).astype(jnp.int32)
    place_ref[...] = owner * CAP + slot

    pl.semaphore_wait(barrier, nx + ny - 2)
    lax.fori_loop(1, nx, tell_column, 0)

    weighed = jnp.concatenate(
        [
            (member * (element // 32).astype(F32)).astype(BF16),
            (member * lax.rem(element, 32).astype(F32)).astype(BF16),
        ],
        axis=0,
    )
    slot_of = onehot(iota((CY, count), 0) == slot)
    both = lax.dot_general(weighed, slot_of, (((1,), (1,)), ((), ())), preferred_element_type=F32)
    send_ids[...] = (32.0 * both[:tiles] + both[tiles:]).reshape(nx, ny, 1, CY)

    loads[2].wait()
    high, low = halves(rows_ref[...])
    split_ref[:, :CY] = high
    split_ref[:, CY:] = low

    pl.semaphore_wait(ready_sem, nx - 1)

    def send_ids_down(turn, carry):
        to = in_column(turn)
        pltpu.make_async_remote_copy(
            src_ref=send_ids.at[to[0]], dst_ref=column_ids.at[turn],
            send_sem=column_send_sem, recv_sem=column_recv_sem,
            device_id=to, device_id_type=MESH,
        ).start()
        return carry

    lax.fori_loop(1, nx, send_ids_down, 0)
    column_ids[0] = send_ids[gx]

    def send_ids_along(turn, carry):
        to = in_line(turn)
        pltpu.make_async_remote_copy(
            src_ref=column_ids.at[:, to[1]], dst_ref=got_ids.at[:, turn],
            send_sem=ids_send_sem, recv_sem=ids_recv_sem,
            device_id=to, device_id_type=MESH,
        ).start()
        return carry

    def pack_rows(turn, carry):
        tile_x = lax.rem(gx + turn, nx)
        wanted = tile_x * group + iota((group, count), 0)
        picked = product(onehot(wanted == place_ref[...]), split_ref[...])
        send_rows[pl.ds(tile_x * ny, ny)] = (picked[:, :CY] + picked[:, CY:]).reshape(ny, CAP, CY)

        def send(turn_y, carry):
            tile_y = lax.rem(gy + turn_y, ny)
            pltpu.make_async_remote_copy(
                src_ref=send_rows.at[tile_x * ny + tile_y], dst_ref=got_rows.at[turn * ny + turn_y],
                send_sem=rows_send_sem, recv_sem=rows_recv_sem.at[turn],
                device_id=(tile_x, tile_y), device_id_type=MESH,
            ).start()
            return carry

        @pl.when(turn == 0)
        def _():
            lax.fori_loop(1, ny, send, 0)

        @pl.when(turn > 0)
        def _():
            lax.fori_loop(0, ny, send, 0)

        return carry

    lax.fori_loop(0, 2, pack_rows, 0)
    from_column = pl.ds(1, nx - 1)
    pltpu.make_async_copy(column_ids.at[from_column], column_ids.at[from_column], column_recv_sem).wait()
    lax.fori_loop(1, ny, send_ids_along, 0)
    got_ids[:, 0] = column_ids[:, gy]
    lax.fori_loop(2, nx, pack_rows, 0)
    got_rows[0] = send_rows[gx * ny + gy]

    zeros = jnp.zeros((ROWS, CY), F32)
    for hand, slab_at, group_at in ((-1, 0, 0), (1, CX + 1, 3)):

        @pl.when(jnp.logical_not(has[hand][0]))
        def _(slab_at=slab_at, group_at=group_at):
            stress[slab_at] = jnp.zeros(SLAB, F32)
            for sweep in range(SWEEPS):
                for c in range(3):
                    fields[sweep, c, slab_at] = jnp.zeros(SLAB, F32)
                    for side_at in range(2):
                        got_ends[sweep, side_at, c, group_at] = zeros

        @pl.when(jnp.logical_not(has[hand][1]))
        def _(side_at=(hand + 1) // 2):
            got_stress_ends[side_at] = jnp.zeros((2, ROWS, CY), F32)
            for sweep in range(SWEEPS):
                for c in range(3):
                    got_ends[sweep, side_at, c] = jnp.zeros((4, ROWS, CY), F32)

    row, column = iota((2 * CY, 2 * CY), 0), iota((2 * CY, 2 * CY), 1)
    k, z = lax.rem(row, CY), lax.rem(column, CY)
    off = jnp.where(k // NZ == z // NZ, k - z, 2)
    after, before = jnp.where(off == 1, 1.0, 0.0), jnp.where(off == -1, 1.0, 0.0)
    sums = jnp.where(off == 0, 2.0, after + before)
    along_matrix[...] = jnp.where(column < CY, sums, after - before).astype(BF16)

    first_half = iota((2 * NZ // 2, CY), 1) < HALF

    def slabs_of(pair, at):
        turned = pair.T
        begin, end = turned[:NZ], turned[NZ:]
        slabs = []
        for odd, values in enumerate(
            (jnp.where(first_half, begin, turn_halves(end)), jnp.where(first_half, turn_halves(begin), end))
        ):
            turning[2 * at + odd] = values
            slabs.append(jnp.stack([turning[2 * at + odd, pl.ds(part, ROWS, stride=PARTS), :] for part in range(PARTS)]))
        return slabs

    def pair_of_slabs(slabs, at):
        for odd in range(2):
            for part in range(PARTS):
                turning[2 * at + odd, pl.ds(part, ROWS, stride=PARTS), :] = slabs[odd][part]
        even, odd = turning[2 * at], turning[2 * at + 1]
        return jnp.concatenate(
            [jnp.where(first_half, even, turn_halves(odd)), jnp.where(first_half, turn_halves(even), odd)], axis=0
        ).T

    def rows_of(x, part):
        return pl.ds(part * ROWS * CX + x, ROWS, stride=CX)

    def take(ref, i):
        return jnp.concatenate([ref[rows_of(2 * i + odd, part), :] for odd in range(2) for part in range(NZ // ROWS)], axis=0)

    def slice_up(slab, at):
        high, low = halves(slab.reshape(NZ, CY))
        sliced[at, :, :CY] = high
        sliced[at, :, CY:] = low

    def merge_ends(from_left, from_right):
        return turn_halves(jnp.where(in_first_half(), from_right, from_left))

    def face(sweep, a):
        mine, theirs = (1, CX + 1) if a < 0 else (CX, 0)
        return pltpu.make_async_remote_copy(
            src_ref=fields.at[sweep, :, mine], dst_ref=fields.at[sweep, :, theirs],
            send_sem=face_send.at[sweep, (a + 1) // 2], recv_sem=face_recv.at[sweep, (1 - a) // 2],
            device_id=(gx + a, gy), device_id_type=MESH,
        )

    def side(sweep, b):
        return pltpu.make_async_remote_copy(
            src_ref=packed.at[sweep], dst_ref=got_ends.at[sweep, (1 - b) // 2, :, pl.ds(1, 2)],
            send_sem=side_send.at[sweep, (b + 1) // 2], recv_sem=side_recv.at[sweep, (1 - b) // 2],
            device_id=(gx, gy + b), device_id_type=MESH,
        )

    def corner(sweep, a, b):
        mine, theirs = (0, 3) if a < 0 else (1, 0)
        return pltpu.make_async_remote_copy(
            src_ref=packed.at[sweep, :, mine], dst_ref=got_ends.at[sweep, (1 - b) // 2, :, theirs],
            send_sem=corner_send.at[sweep, a + 1 + (b + 1) // 2], recv_sem=corner_recv.at[sweep, 1 - a + (1 - b) // 2],
            device_id=(gx + a, gy + b), device_id_type=MESH,
        )

    def stress_face(a):
        mine, theirs = (1, CX + 1) if a < 0 else (CX, 0)
        return pltpu.make_async_remote_copy(
            src_ref=stress.at[mine], dst_ref=stress.at[theirs],
            send_sem=stress_face_send.at[(a + 1) // 2], recv_sem=stress_face_recv.at[(1 - a) // 2],
            device_id=(gx + a, gy), device_id_type=MESH,
        )

    def stress_side(b):
        return pltpu.make_async_remote_copy(
            src_ref=packed_stress, dst_ref=got_stress_ends.at[(1 - b) // 2],
            send_sem=stress_side_send.at[(b + 1) // 2], recv_sem=stress_side_recv.at[(1 - b) // 2],
            device_id=(gx, gy + b), device_id_type=MESH,
        )

    pair_of = (-1, 1)

    def faces(sweep):
        return [((a, 0), lambda a=a: face(sweep, a)) for a in pair_of]

    def edges(sweep):
        return [((0, b), lambda b=b: side(sweep, b)) for b in pair_of] + [
            ((a, b), lambda a=a, b=b: corner(sweep, a, b)) for a in pair_of for b in pair_of
        ]

    stress_faces = [((a, 0), lambda a=a: stress_face(a)) for a in pair_of]
    stress_sides = [((0, b), lambda b=b: stress_side(b)) for b in pair_of]

    def arrival(ref, sem):
        return lambda: pltpu.make_async_copy(ref, ref, sem)

    def from_faces(sweep):
        return [
            ((a, 0), arrival(fields.at[sweep, :, 0 if a < 0 else CX + 1], face_recv.at[sweep, (a + 1) // 2]))
            for a in pair_of
        ]

    def from_edges(sweep):
        return [
            ((0, b), arrival(got_ends.at[sweep, (b + 1) // 2, :, pl.ds(1, 2)], side_recv.at[sweep, (b + 1) // 2]))
            for b in pair_of
        ] + [
            (
                (a, b),
                arrival(
                    got_ends.at[sweep, (b + 1) // 2, :, 0 if a < 0 else 3],
                    corner_recv.at[sweep, a + 1 + (b + 1) // 2],
                ),
            )
            for a in pair_of
            for b in pair_of
        ]

    from_stress_faces = [
        ((a, 0), arrival(stress.at[0 if a < 0 else CX + 1], stress_face_recv.at[(a + 1) // 2])) for a in pair_of
    ]
    from_stress_sides = [
        ((0, b), arrival(got_stress_ends.at[(b + 1) // 2], stress_side_recv.at[(b + 1) // 2])) for b in pair_of
    ]

    def start(copy):
        copy.start()

    def receive(copy):
        copy.wait()

    def finish(copy):
        copy.wait_send()

    def along_own(sweep):
        for c in range(3):
            at = pl.ds(c * SLABS + 1, CX)
            both = product(sliced[at].reshape(CX * NZ, 2 * CY), along_matrix[...])
            summed[at] = both[:, :CY].reshape((CX,) + SLAB)
            differed[at] = both[:, CY:].reshape((CX,) + SLAB)

    def along_halo(sweep):
        over(from_edges(sweep) + from_faces(sweep), receive)
        for c in range(3):
            for g in range(4):
                at = pl.ds(g * ROWS, ROWS)
                ends[c, at] = merge_ends(got_ends[sweep, 0, c, g], got_ends[sweep, 1, c, g])
        halo = [fields[sweep, c, at].reshape(NZ, CY) for c in range(3) for at in (0, CX + 1)]
        high, low = halves(jnp.concatenate(halo + [ends[c] for c in range(3)], axis=0))
        both = product(jnp.concatenate([high, low], axis=1), along_matrix[...])
        for c in range(3):
            for hand, at in enumerate((0, CX + 1)):
                first = (2 * c + hand) * NZ
                summed[c * SLABS + at] = both[first : first + NZ, :CY].reshape(SLAB)
                differed[c * SLABS + at] = both[first : first + NZ, CY:].reshape(SLAB)
            first = 6 * NZ + c * 4 * ROWS
            ends_summed[c] = both[first : first + 4 * ROWS, :CY]
            ends_differed[c] = both[first : first + 4 * ROWS, CY:]

        def near(ref, c, step):
            return ref[c, pl.ds(ROWS + step, CX), :]

        for c in range(3):
            around = (near(ends_summed, c, -1) + near(ends_summed, c, 1)) + 2.0 * near(ends_summed, c, 0)
            if c == 0:
                across = near(ends_differed, 2, 0)
            elif c == 1:
                across = near(ends, 2, 1) - near(ends, 2, -1)
            else:
                across = near(ends_differed, 0, 0) + (near(ends, 1, 1) - near(ends, 1, -1))
            sign = jnp.where(iota((CX, CY), 1) < HALF, -COUPLING, COUPLING)
            ends_added[c] = around + sign * across

    def rest(sweep, x, c):
        at = x + 1

        def field(component, to):
            return fields[sweep, component, to]

        def along_sum(to):
            return summed[c * SLABS + to]

        def along_difference(component, to):
            return differed[component * SLABS + to]

        around = (along_sum(at - 1) + along_sum(at + 1)) + 2.0 * along_sum(at)
        if c == 0:
            across = along_difference(2, at)
        elif c == 1:
            across = field(2, at + 1) - field(2, at - 1)
        else:
            across = along_difference(0, at) + (field(1, at + 1) - field(1, at - 1))
        across = COUPLING * across
        added = ends_added[c, pl.ds(x, 1), :]
        total_around = (up(around + across, added) + down(around - across, added)) + 2.0 * around
        if c < 2:
            total_around = total_around + COUPLING * (along_difference(1 - c, at + 1) - along_difference(1 - c, at - 1))
        return (0.25 / DIAGONAL_WEIGHT) * total_around - ((DIAGONAL_WEIGHT + 2.0) / DIAGONAL_WEIGHT) * field(c, at)

    loads[3].wait()

    def store_ends(slab, x, ref):
        ref[x // ROWS, pl.ds(lax.rem(x, ROWS), 1), :] = end_row(slab)

    def begin(i, carry):
        for c in range(3):
            for odd, slab in enumerate(slabs_of(take(start_ref.at[c], i), c)):
                x = 2 * i + odd
                fields[0, c, x + 1] = slab
                slice_up(slab, c * SLABS + x + 1)
                store_ends(slab, x, packed.at[0, c])
        return carry

    lax.fori_loop(0, CX // 2, begin, 0)
    over(faces(0), start)
    over(edges(0), start)

    loads[4].wait()
    loads[5].wait()

    def material(i, carry):
        for odd, modulus in enumerate(slabs_of(take(modulus_ref, i), 0)):
            x = 2 * i + odd
            stress[x + 1] = modulus
            inverse[x] = 1.0 / (DIAGONAL_WEIGHT * modulus)
        for odd, birth in enumerate(slabs_of(take(birth_ref, i).astype(F32), 1)):
            born[2 * i + odd] = birth
        return carry

    lax.fori_loop(0, CX // 2, material, 0)
    along_own(0)

    lower = jnp.full((ROWS, CY), bounds_ref[0], F32)
    upper = jnp.full((ROWS, CY), bounds_ref[1], F32)
    theta = (upper + lower) / 2.0
    delta = (upper - lower) / 2.0
    sigma = theta / delta
    ratio = 1.0 / sigma

    along_halo(0)

    def first_rest(x, carry):
        for c in range(3):
            steps[c, x] = rest(0, x, c)
        return carry

    lax.fori_loop(0, CX, first_rest, 0, unroll=2)

    others = pl.ds(1, tiles - 1)
    from_line = pl.ds(1, ny - 1)
    pltpu.make_async_copy(got_ids.at[:, from_line], got_ids.at[:, from_line], ids_recv_sem).wait()
    spread = onehot(iota((CY, group), 0) == lax.rem(iota((CY, group), 1), CAP))
    own_lane = iota((ny, group), 0) == iota((ny, group), 1) // CAP
    total[...] = jnp.zeros_like(total)

    def collect(turn, carry):
        @pl.when(turn == 0)
        def _():
            part = got_rows.at[pl.ds(1, ny - 1)]
            pltpu.make_async_copy(part, part, rows_recv_sem.at[0]).wait()

        @pl.when(turn > 0)
        def _():
            part = got_rows.at[pl.ds(turn * ny, ny)]
            pltpu.make_async_copy(part, part, rows_recv_sem.at[turn]).wait()

        ids = got_ids[turn].reshape(ny, CY)
        ids_high = jnp.floor(ids * (1.0 / 32.0))
        ids_low = ids - 32.0 * ids_high
        wide = 32.0 * product(ids_high.astype(BF16), spread) + product(ids_low.astype(BF16), spread)
        flat = jnp.sum(jnp.where(own_lane, wide, 0.0), axis=0, keepdims=True).astype(jnp.int32) - 1
        place = onehot(iota((CELLS, group), 0) == flat)
        high, low = halves(got_rows[pl.ds(turn * ny, ny)].reshape(group, CY))
        total[...] += product(place, jnp.concatenate([high, low], axis=1))
        return carry

    lax.fori_loop(0, nx, collect, 0)

    def strain(i, carry):
        at = pl.ds(2 * i * NZ, 2 * NZ)
        for odd, slab in enumerate(slabs_of(total[at, :CY] + total[at, CY:], 0)):
            x = 2 * i + odd
            slab = stress[x + 1] * slab
            stress[x + 1] = slab
            slice_up(slab, x + 1)
            store_ends(slab, x, packed_stress)
        return carry

    lax.fori_loop(0, CX // 2, strain, 0)
    over(stress_faces, start)
    over(stress_sides, start)
    at = pl.ds(1, CX)
    differed[at] = product(sliced[at].reshape(CX * NZ, 2 * CY), along_matrix[:, CY:]).reshape((CX,) + SLAB)
    over(from_stress_sides, receive)
    for g in range(2):
        ends[0, pl.ds(g * ROWS, ROWS)] = merge_ends(got_stress_ends[0, g], got_stress_ends[1, g])
    over(from_stress_faces, receive)

    def keep_moved(sweep, x, c, moved, step):
        at = x + 1
        steps[c, x] = step
        fields[sweep + 1, c, at] = moved
        slice_up(moved, c * SLABS + at)
        store_ends(moved, x, packed.at[sweep + 1, c])

    def softer(sweep, x):
        return jnp.where(born[x] <= sweep, 1.0, 1.0 / SOFTENED)

    first_gain = 1.0 / theta

    def first_move(x):
        middle = stress[x + 1]
        scale = 0.5 * inverse[x]
        soft = softer(0, x)
        added = ends[0, pl.ds(x, 1), :]
        gradients = (differed[x + 1], stress[x + 2] - stress[x], up(middle, added) - down(middle, added))
        for c, gradient in enumerate(gradients):
            force = scale * gradient
            forces[c, x] = force
            step = first_gain * (steps[c, x] + soft * force)
            keep_moved(0, x, c, fields[0, c, x + 1] + step, step)

    def ends_first(move, sweep):
        lax.fori_loop(0, 2, lambda i, carry: (move(i * (CX - 1)), carry)[1], 0, unroll=2)
        over(faces(sweep + 1), start)
        lax.fori_loop(1, CX - 1, lambda x, carry: (move(x), carry)[1], 0, unroll=2)
        over(edges(sweep + 1), start)
        along_own(sweep + 1)

    ends_first(first_move, 0)

    for sweep in range(1, SWEEPS):
        ratio_next = 1.0 / (2.0 * sigma - ratio)
        keep = ratio_next * ratio
        gain = 2.0 * ratio_next / delta
        ratio = ratio_next
        along_halo(sweep)

        def moves(x, sweep=sweep, keep=keep, gain=gain):
            soft = softer(sweep, x)
            for c in range(3):
                step = gain * (rest(sweep, x, c) + soft * forces[c, x]) + keep * steps[c, x]
                yield c, fields[sweep, c, x + 1] + step, step

        if sweep < SWEEPS - 1:

            def move(x, sweep=sweep, moves=moves):
                for c, moved, step in moves(x):
                    keep_moved(sweep, x, c, moved, step)

            ends_first(move, sweep)
        else:

            def last(i, carry, moves=moves):
                both = [[moved for _, moved, _ in moves(2 * i + odd)] for odd in range(2)]
                for c in range(3):
                    block = pair_of_slabs([both[0][c], both[1][c]], c)
                    for odd in range(2):
                        for part in range(NZ // ROWS):
                            first = odd * NZ + part * ROWS
                            out_ref[c, rows_of(2 * i + odd, part), :] = block[first : first + ROWS]
                return carry

            lax.fori_loop(0, CX // 2, last, 0)

    pltpu.make_async_copy(column_ids.at[from_column], column_ids.at[from_column], column_send_sem).wait()
    pltpu.make_async_copy(got_ids.at[:, from_line], got_ids.at[:, from_line], ids_send_sem).wait()
    pltpu.make_async_copy(send_rows.at[others], send_rows.at[others], rows_send_sem).wait()
    over(stress_faces + stress_sides, finish)
    for sweep in range(SWEEPS):
        over(edges(sweep) + faces(sweep), finish)


def local(thermal_rows, row_owner, row_element, modulus, birth, start_disp, bounds):
    nx, ny = lax.axis_size("gx"), lax.axis_size("gy")
    tiles = nx * ny
    count = thermal_rows.shape[0]
    vmem, dma = pltpu.VMEM, pltpu.SemaphoreType.DMA
    moved = pl.pallas_call(
        functools.partial(kernel, nx, ny),
        out_shape=jax.ShapeDtypeStruct((3, CELLS, CY), F32),
        in_specs=[pl.BlockSpec(memory_space=pl.ANY)] * 6 + [pl.BlockSpec(memory_space=pltpu.SMEM)],
        out_specs=pl.BlockSpec(memory_space=pltpu.VMEM),
        scratch_shapes=[
            vmem((1, count), jnp.int32),
            vmem((1, count), jnp.int32),
            vmem((count, CY), F32),
            vmem((CELLS, CY), F32),
            vmem((CELLS, CY), jnp.int32),
            vmem((3, CELLS, CY), F32),
            dma((6,)),
            vmem((count, 2 * CY), BF16),
            vmem((1, count), jnp.int32),
            vmem((tiles, CAP, CY), F32),
            vmem((nx, ny, 1, CY), F32),
            vmem((nx, ny, 1, CY), F32),
            vmem((tiles, CAP, CY), F32),
            vmem((nx, ny, 1, CY), F32),
            vmem((CELLS, 2 * CY), F32),
            pltpu.SemaphoreType.REGULAR,
            dma, dma, dma, dma, dma, dma((nx,)),
            vmem((SWEEPS, 3, SLABS) + SLAB, F32),
            vmem((SLABS,) + SLAB, F32),
            vmem((CX,) + SLAB, F32),
            vmem((3, CX) + SLAB, F32),
            vmem((CX,) + SLAB, F32),
            vmem((3, CX) + SLAB, F32),
            vmem((3 * SLABS,) + SLAB, F32),
            vmem((3 * SLABS,) + SLAB, F32),
            vmem((3 * SLABS, NZ, 2 * CY), BF16),
            vmem((2 * CY, 2 * CY), BF16),
            vmem((6, NZ, CY), F32),
            vmem((SWEEPS, 3, 2, ROWS, CY), F32),
            vmem((2, ROWS, CY), F32),
            vmem((SWEEPS, 2, 3, 4, ROWS, CY), F32),
            vmem((2, 2, ROWS, CY), F32),
            vmem((3, 4 * ROWS, CY), F32),
            vmem((3, 4 * ROWS, CY), F32),
            vmem((3, 4 * ROWS, CY), F32),
            vmem((3, CX, CY), F32),
            dma((SWEEPS, 2)), dma((SWEEPS, 2)), dma((SWEEPS, 2)), dma((SWEEPS, 2)), dma((SWEEPS, 4)), dma((SWEEPS, 4)),
            dma((2,)), dma((2,)), dma((2,)), dma((2,)),
        ],
        compiler_params=pltpu.CompilerParams(
            collective_id=0, has_side_effects=True, vmem_limit_bytes=60 * 1024 * 1024
        ),
        name="weld",
    )(
        row_owner.reshape(1, count), row_element.reshape(1, count), thermal_rows,
        modulus.reshape(CELLS, CY), birth.reshape(CELLS, CY), start_disp.reshape(3, CELLS, CY), bounds,
    )
    return moved.reshape(start_disp.shape)


def solution(mesh):
    placed = (
        P(("gx", "gy"), None),
        P(("gx", "gy"), None),
        P(("gx", "gy"), None),
        P(None, "gx", "gy"),
        P(None, "gx", "gy"),
        P(None, None, "gx", "gy"),
        P(),
    )
    return jax.shard_map(
        local, mesh=mesh, in_specs=placed, out_specs=P(None, None, "gx", "gy"), check_vma=False
    )
```

```python
import functools

import jax
import jax.numpy as jnp
from jax import lax
from jax.experimental import pallas as pl
from jax.experimental.pallas import tpu as pltpu
from jax.sharding import PartitionSpec as P

SWEEPS = 4
CAP = 24
FIRST = 2
SECOND = 4
NZ = 64
CX = 16
CY = 128
ROWS = 8
PARTS = 8
HALF = CY // 2
CELLS = NZ * CX
SLABS = CX + 2
SLAB = (PARTS, ROWS, CY)
DIAGONAL_WEIGHT = 14.5
COUPLING = 0.25
SOFTENED = 0.05

MESH = pl.DeviceIdType.MESH
F32 = jnp.float32
BF16 = jnp.bfloat16


def halves(values):
    high = values.astype(BF16)
    low = (values - high.astype(F32)).astype(BF16)
    return high, low


def onehot(matches):
    return jnp.where(matches, 1.0, 0.0).astype(BF16)


def iota(shape, dim):
    return lax.broadcasted_iota(jnp.int32, shape, dim)


def product(left, right):
    return jnp.dot(left, right, preferred_element_type=F32)


def row_index():
    return iota((ROWS, CY), 0)


def in_first_half():
    return iota((ROWS, CY), 1) < HALF


def up(slab, ends):
    first = pltpu.roll(slab[0], ROWS - 1, 0)
    turned = jnp.where(in_first_half(), pltpu.roll(first, HALF, 1), ends)
    return jnp.concatenate([slab[1:], jnp.where(row_index() == ROWS - 1, turned, first)[None]], axis=0)


def down(slab, ends):
    last = pltpu.roll(slab[PARTS - 1], 1, 0)
    turned = jnp.where(in_first_half(), ends, pltpu.roll(last, HALF, 1))
    return jnp.concatenate([jnp.where(row_index() == 0, turned, last)[None], slab[:-1]], axis=0)


def end_row(slab):
    return jnp.where(iota((1, CY), 1) < HALF, slab[0][:1], pltpu.roll(slab[PARTS - 1], 1, 0)[:1])


def turn_halves(values):
    return pltpu.roll(values, HALF, 1)


def kernel(
    nx, ny,
    owner_hbm, element_hbm, rows_hbm, modulus_hbm, birth_hbm, start_hbm, bounds_ref,
    out_ref,
    owner_ref, element_ref, rows_ref, modulus_ref, birth_ref, start_ref, in_sem,
    split_ref, place_ref, send_rows, send_ids, column_ids, got_rows, got_ids, total,
    ready_sem, column_send_sem, column_recv_sem, ids_send_sem, ids_recv_sem, rows_send_sem, rows_recv_sem,
    fields, stress, inverse, forces, born, steps, summed, differed, sliced,
    along_matrix, turning,
    packed, packed_stress, got_ends, got_stress_ends, ends, ends_summed, ends_differed, ends_added,
    face_send, face_recv, side_send, side_recv, corner_send, corner_recv,
    stress_face_send, stress_face_recv, stress_side_send, stress_side_recv,
):
    tiles = nx * ny
    count = rows_ref.shape[0]
    group = ny * CAP
    gx = lax.axis_index("gx")
    gy = lax.axis_index("gy")

    loads = [
        pltpu.make_async_copy(source, target, in_sem.at[i])
        for i, (source, target) in enumerate(
            [
                (owner_hbm, owner_ref), (element_hbm, element_ref), (rows_hbm, rows_ref),
                (start_hbm, start_ref), (modulus_hbm, modulus_ref), (birth_hbm, birth_ref),
            ]
        )
    ]
    for load in loads:
        load.start()

    def in_column(turn):
        return lax.rem(gx + turn, nx), gy

    def in_line(turn):
        return gx, lax.rem(gy + turn, ny)

    barrier = pltpu.get_barrier_semaphore()

    def greet_line(turn, carry):
        pl.semaphore_signal(barrier, inc=1, device_id=in_line(turn), device_id_type=MESH)
        return carry

    def greet_column(turn, carry):
        pl.semaphore_signal(barrier, inc=1, device_id=in_column(turn), device_id_type=MESH)
        return carry

    def tell_column(turn, carry):
        pl.semaphore_signal(ready_sem, inc=1, device_id=in_column(turn), device_id_type=MESH)
        return carry

    lax.fori_loop(1, ny, greet_line, 0)
    lax.fori_loop(1, nx, greet_column, 0)

    has = {-1: (gx > 0, gy > 0), 1: (gx < nx - 1, gy < ny - 1)}

    def present(a, b):
        if a == 0:
            return has[b][1]
        if b == 0:
            return has[a][0]
        return jnp.logical_and(has[a][0], has[b][1])

    def over(copies, do):
        for where, copy in copies:

            @pl.when(present(*where))
            def _(copy=copy):
                do(copy())

    loads[0].wait()
    loads[1].wait()
    owner = owner_ref[...]
    given = element_ref[...]
    depth_index = given // CX
    element = lax.rem(given, CX) * NZ + depth_index + 1
    member = jnp.where(iota((tiles, count), 0) == owner, 1.0, 0.0)
    member16 = member.astype(BF16)
    block = 256
    earlier = onehot(iota((block, block), 0) < iota((block, block), 1))
    carried = jnp.zeros((tiles, 1), F32)
    slots = []
    for first in range(0, count, block):
        part = member[:, first : first + block]
        before = product(member16[:, first : first + block], earlier) + carried
        slots.append(jnp.sum(before * part, axis=0, keepdims=True))
        carried = carried + jnp.sum(part, axis=1, keepdims=True)
    slot = jnp.concatenate(slots, axis=1).astype(jnp.int32)
    place_ref[...] = owner * CAP + slot

    pl.semaphore_wait(barrier, nx + ny - 2)
    lax.fori_loop(1, nx, tell_column, 0)

    loads[2].wait()
    high, low = halves(rows_ref[...])
    split_ref[:, :CY] = high
    split_ref[:, CY:] = low

    pl.semaphore_wait(ready_sem, nx - 1)

    def pack_rows(turn, carry):
        tile_x = lax.rem(gx + turn, nx)
        wanted = tile_x * group + iota((group, count), 0)
        picked = product(onehot(wanted == place_ref[...]), split_ref[...])
        send_rows[pl.ds(tile_x * ny, ny)] = (picked[:, :CY] + picked[:, CY:]).reshape(ny, CAP, CY)

        def send(turn_y, carry):
            tile_y = lax.rem(gy + turn_y, ny)
            pltpu.make_async_remote_copy(
                src_ref=send_rows.at[tile_x * ny + tile_y], dst_ref=got_rows.at[turn * ny + turn_y],
                send_sem=rows_send_sem, recv_sem=rows_recv_sem.at[turn],
                device_id=(tile_x, tile_y), device_id_type=MESH,
            ).start()
            return carry

        @pl.when(turn == 0)
        def _():
            lax.fori_loop(1, ny, send, 0)

        @pl.when(turn > 0)
        def _():
            lax.fori_loop(0, ny, send, 0)

        return carry

    lax.fori_loop(0, FIRST, pack_rows, 0)

    weighed = jnp.concatenate(
        [
            (member * (element // 32).astype(F32)).astype(BF16),
            (member * lax.rem(element, 32).astype(F32)).astype(BF16),
        ],
        axis=0,
    )
    slot_of = onehot(iota((CY, count), 0) == slot)
    both = lax.dot_general(weighed, slot_of, (((1,), (1,)), ((), ())), preferred_element_type=F32)
    send_ids[...] = (32.0 * both[:tiles] + both[tiles:]).reshape(nx, ny, 1, CY)

    def send_ids_down(turn, carry):
        to = in_column(turn)
        pltpu.make_async_remote_copy(
            src_ref=send_ids.at[to[0]], dst_ref=column_ids.at[turn],
            send_sem=column_send_sem, recv_sem=column_recv_sem,
            device_id=to, device_id_type=MESH,
        ).start()
        return carry

    lax.fori_loop(1, nx, send_ids_down, 0)
    column_ids[0] = send_ids[gx]

    def send_ids_along(turn, carry):
        to = in_line(turn)
        pltpu.make_async_remote_copy(
            src_ref=column_ids.at[:, to[1]], dst_ref=got_ids.at[:, turn],
            send_sem=ids_send_sem, recv_sem=ids_recv_sem,
            device_id=to, device_id_type=MESH,
        ).start()
        return carry

    zeros = jnp.zeros((ROWS, CY), F32)
    for hand, slab_at, group_at in ((-1, 0, 0), (1, CX + 1, 3)):

        @pl.when(jnp.logical_not(has[hand][0]))
        def _(slab_at=slab_at, group_at=group_at):
            stress[slab_at] = jnp.zeros(SLAB, F32)
            for sweep in range(SWEEPS):
                for c in range(3):
                    fields[sweep, c, slab_at] = jnp.zeros(SLAB, F32)
                    for side_at in range(2):
                        got_ends[sweep, side_at, c, group_at] = zeros

        @pl.when(jnp.logical_not(has[hand][1]))
        def _(side_at=(hand + 1) // 2):
            got_stress_ends[side_at] = jnp.zeros((2, ROWS, CY), F32)
            for sweep in range(SWEEPS):
                for c in range(3):
                    got_ends[sweep, side_at, c] = jnp.zeros((4, ROWS, CY), F32)

    row, column = iota((2 * CY, 2 * CY), 0), iota((2 * CY, 2 * CY), 1)
    k, z = lax.rem(row, CY), lax.rem(column, CY)
    off = jnp.where(k // NZ == z // NZ, k - z, 2)
    after, before = jnp.where(off == 1, 1.0, 0.0), jnp.where(off == -1, 1.0, 0.0)
    sums = jnp.where(off == 0, 2.0, after + before)
    along_matrix[...] = jnp.where(column < CY, sums, after - before).astype(BF16)

    first_half = iota((2 * NZ // 2, CY), 1) < HALF

    def slabs_of(pair, at):
        turned = pair.T
        begin, end = turned[:NZ], turned[NZ:]
        slabs = []
        for odd, values in enumerate(
            (jnp.where(first_half, begin, turn_halves(end)), jnp.where(first_half, turn_halves(begin), end))
        ):
            turning[2 * at + odd] = values
            slabs.append(jnp.stack([turning[2 * at + odd, pl.ds(part, ROWS, stride=PARTS), :] for part in range(PARTS)]))
        return slabs

    def pair_of_slabs(slabs, at):
        for odd in range(2):
            for part in range(PARTS):
                turning[2 * at + odd, pl.ds(part, ROWS, stride=PARTS), :] = slabs[odd][part]
        even, odd = turning[2 * at], turning[2 * at + 1]
        return jnp.concatenate(
            [jnp.where(first_half, even, turn_halves(odd)), jnp.where(first_half, turn_halves(even), odd)], axis=0
        ).T

    def rows_of(x, part):
        return pl.ds(part * ROWS * CX + x, ROWS, stride=CX)

    def take(ref, i):
        return jnp.concatenate([ref[rows_of(2 * i + odd, part), :] for odd in range(2) for part in range(NZ // ROWS)], axis=0)

    def slice_up(slab, at):
        high, low = halves(slab.reshape(NZ, CY))
        sliced[at, :, :CY] = high
        sliced[at, :, CY:] = low

    def merge_ends(from_left, from_right):
        return turn_halves(jnp.where(in_first_half(), from_right, from_left))

    def face(sweep, a):
        mine, theirs = (1, CX + 1) if a < 0 else (CX, 0)
        return pltpu.make_async_remote_copy(
            src_ref=fields.at[sweep, :, mine], dst_ref=fields.at[sweep, :, theirs],
            send_sem=face_send.at[sweep, (a + 1) // 2], recv_sem=face_recv.at[sweep, (1 - a) // 2],
            device_id=(gx + a, gy), device_id_type=MESH,
        )

    def side(sweep, b):
        return pltpu.make_async_remote_copy(
            src_ref=packed.at[sweep], dst_ref=got_ends.at[sweep, (1 - b) // 2, :, pl.ds(1, 2)],
            send_sem=side_send.at[sweep, (b + 1) // 2], recv_sem=side_recv.at[sweep, (1 - b) // 2],
            device_id=(gx, gy + b), device_id_type=MESH,
        )

    def corner(sweep, a, b):
        mine, theirs = (0, 3) if a < 0 else (1, 0)
        return pltpu.make_async_remote_copy(
            src_ref=packed.at[sweep, :, mine], dst_ref=got_ends.at[sweep, (1 - b) // 2, :, theirs],
            send_sem=corner_send.at[sweep, a + 1 + (b + 1) // 2], recv_sem=corner_recv.at[sweep, 1 - a + (1 - b) // 2],
            device_id=(gx + a, gy + b), device_id_type=MESH,
        )

    def stress_face(a):
        mine, theirs = (1, CX + 1) if a < 0 else (CX, 0)
        return pltpu.make_async_remote_copy(
            src_ref=stress.at[mine], dst_ref=stress.at[theirs],
            send_sem=stress_face_send.at[(a + 1) // 2], recv_sem=stress_face_recv.at[(1 - a) // 2],
            device_id=(gx + a, gy), device_id_type=MESH,
        )

    def stress_side(b):
        return pltpu.make_async_remote_copy(
            src_ref=packed_stress, dst_ref=got_stress_ends.at[(1 - b) // 2],
            send_sem=stress_side_send.at[(b + 1) // 2], recv_sem=stress_side_recv.at[(1 - b) // 2],
            device_id=(gx, gy + b), device_id_type=MESH,
        )

    pair_of = (-1, 1)

    def faces(sweep):
        return [((a, 0), lambda a=a: face(sweep, a)) for a in pair_of]

    def edges(sweep):
        return [((0, b), lambda b=b: side(sweep, b)) for b in pair_of] + [
            ((a, b), lambda a=a, b=b: corner(sweep, a, b)) for a in pair_of for b in pair_of
        ]

    stress_faces = [((a, 0), lambda a=a: stress_face(a)) for a in pair_of]
    stress_sides = [((0, b), lambda b=b: stress_side(b)) for b in pair_of]

    def arrival(ref, sem):
        return lambda: pltpu.make_async_copy(ref, ref, sem)

    def from_faces(sweep):
        return [
            ((a, 0), arrival(fields.at[sweep, :, 0 if a < 0 else CX + 1], face_recv.at[sweep, (a + 1) // 2]))
            for a in pair_of
        ]

    def from_edges(sweep):
        return [
            ((0, b), arrival(got_ends.at[sweep, (b + 1) // 2, :, pl.ds(1, 2)], side_recv.at[sweep, (b + 1) // 2]))
            for b in pair_of
        ] + [
            (
                (a, b),
                arrival(
                    got_ends.at[sweep, (b + 1) // 2, :, 0 if a < 0 else 3],
                    corner_recv.at[sweep, a + 1 + (b + 1) // 2],
                ),
            )
            for a in pair_of
            for b in pair_of
        ]

    from_stress_faces = [
        ((a, 0), arrival(stress.at[0 if a < 0 else CX + 1], stress_face_recv.at[(a + 1) // 2])) for a in pair_of
    ]
    from_stress_sides = [
        ((0, b), arrival(got_stress_ends.at[(b + 1) // 2], stress_side_recv.at[(b + 1) // 2])) for b in pair_of
    ]

    def start(copy):
        copy.start()

    def receive(copy):
        copy.wait()

    def finish(copy):
        copy.wait_send()

    def along_own(sweep):
        for c in range(3):
            at = pl.ds(c * SLABS + 1, CX)
            both = product(sliced[at].reshape(CX * NZ, 2 * CY), along_matrix[...])
            summed[at] = both[:, :CY].reshape((CX,) + SLAB)
            differed[at] = both[:, CY:].reshape((CX,) + SLAB)

    def along_halo(sweep):
        over(from_edges(sweep) + from_faces(sweep), receive)
        for c in range(3):
            for g in range(4):
                at = pl.ds(g * ROWS, ROWS)
                ends[c, at] = merge_ends(got_ends[sweep, 0, c, g], got_ends[sweep, 1, c, g])
        halo = [fields[sweep, c, at].reshape(NZ, CY) for c in range(3) for at in (0, CX + 1)]
        high, low = halves(jnp.concatenate(halo + [ends[c] for c in range(3)], axis=0))
        both = product(jnp.concatenate([high, low], axis=1), along_matrix[...])
        for c in range(3):
            for hand, at in enumerate((0, CX + 1)):
                first = (2 * c + hand) * NZ
                summed[c * SLABS + at] = both[first : first + NZ, :CY].reshape(SLAB)
                differed[c * SLABS + at] = both[first : first + NZ, CY:].reshape(SLAB)
            first = 6 * NZ + c * 4 * ROWS
            ends_summed[c] = both[first : first + 4 * ROWS, :CY]
            ends_differed[c] = both[first : first + 4 * ROWS, CY:]

        def near(ref, c, step):
            return ref[c, pl.ds(ROWS + step, CX), :]

        for c in range(3):
            around = (near(ends_summed, c, -1) + near(ends_summed, c, 1)) + 2.0 * near(ends_summed, c, 0)
            if c == 0:
                across = near(ends_differed, 2, 0)
            elif c == 1:
                across = near(ends, 2, 1) - near(ends, 2, -1)
            else:
                across = near(ends_differed, 0, 0) + (near(ends, 1, 1) - near(ends, 1, -1))
            sign = jnp.where(iota((CX, CY), 1) < HALF, -COUPLING, COUPLING)
            ends_added[c] = around + sign * across

    def rest(sweep, x, c):
        at = x + 1

        def field(component, to):
            return fields[sweep, component, to]

        def along_sum(to):
            return summed[c * SLABS + to]

        def along_difference(component, to):
            return differed[component * SLABS + to]

        around = (along_sum(at - 1) + along_sum(at + 1)) + 2.0 * along_sum(at)
        if c == 0:
            across = along_difference(2, at)
        elif c == 1:
            across = field(2, at + 1) - field(2, at - 1)
        else:
            across = along_difference(0, at) + (field(1, at + 1) - field(1, at - 1))
        across = COUPLING * across
        added = ends_added[c, pl.ds(x, 1), :]
        total_around = (up(around + across, added) + down(around - across, added)) + 2.0 * around
        if c < 2:
            total_around = total_around + COUPLING * (along_difference(1 - c, at + 1) - along_difference(1 - c, at - 1))
        return (0.25 / DIAGONAL_WEIGHT) * total_around - ((DIAGONAL_WEIGHT + 2.0) / DIAGONAL_WEIGHT) * field(c, at)

    loads[3].wait()

    def store_ends(slab, x, ref):
        ref[x // ROWS, pl.ds(lax.rem(x, ROWS), 1), :] = end_row(slab)

    def begin(i, carry):
        for c in range(3):
            for odd, slab in enumerate(slabs_of(take(start_ref.at[c], i), c)):
                x = 2 * i + odd
                fields[0, c, x + 1] = slab
                slice_up(slab, c * SLABS + x + 1)
                store_ends(slab, x, packed.at[0, c])
        return carry

    lax.fori_loop(0, CX // 2, begin, 0)
    over(edges(0), start)
    over(faces(0), start)
    lax.fori_loop(FIRST, SECOND, pack_rows, 0)
    from_column = pl.ds(1, nx - 1)
    pltpu.make_async_copy(column_ids.at[from_column], column_ids.at[from_column], column_recv_sem).wait()
    lax.fori_loop(1, ny, send_ids_along, 0)
    got_ids[:, 0] = column_ids[:, gy]
    lax.fori_loop(SECOND, nx, pack_rows, 0)
    got_rows[0] = send_rows[gx * ny + gy]

    loads[4].wait()
    loads[5].wait()

    def material(i, carry):
        for odd, modulus in enumerate(slabs_of(take(modulus_ref, i), 0)):
            x = 2 * i + odd
            stress[x + 1] = modulus
            inverse[x] = 1.0 / (DIAGONAL_WEIGHT * modulus)
        for odd, birth in enumerate(slabs_of(take(birth_ref, i).astype(F32), 1)):
            born[2 * i + odd] = birth
        return carry

    lax.fori_loop(0, CX // 2, material, 0)
    along_own(0)

    lower = jnp.full((ROWS, CY), bounds_ref[0], F32)
    upper = jnp.full((ROWS, CY), bounds_ref[1], F32)
    theta = (upper + lower) / 2.0
    delta = (upper - lower) / 2.0
    sigma = theta / delta
    ratio = 1.0 / sigma

    along_halo(0)

    def first_rest(x, carry):
        for c in range(3):
            steps[c, x] = rest(0, x, c)
        return carry

    lax.fori_loop(0, CX, first_rest, 0, unroll=2)

    others = pl.ds(1, tiles - 1)
    from_line = pl.ds(1, ny - 1)
    pltpu.make_async_copy(got_ids.at[:, from_line], got_ids.at[:, from_line], ids_recv_sem).wait()
    spread = onehot(iota((CY, group), 0) == lax.rem(iota((CY, group), 1), CAP))
    own_lane = iota((ny, group), 0) == iota((ny, group), 1) // CAP
    total[...] = jnp.zeros_like(total)

    def collect(turn, carry):
        @pl.when(turn == 0)
        def _():
            part = got_rows.at[pl.ds(1, ny - 1)]
            pltpu.make_async_copy(part, part, rows_recv_sem.at[0]).wait()

        @pl.when(turn > 0)
        def _():
            part = got_rows.at[pl.ds(turn * ny, ny)]
            pltpu.make_async_copy(part, part, rows_recv_sem.at[turn]).wait()

        part = got_rows.at[pl.ds((turn + 1) * ny, ny)]
        pltpu.make_async_copy(part, part, rows_recv_sem.at[turn + 1]).wait()
        places = []
        for at in range(2):
            ids = got_ids[turn + at].reshape(ny, CY)
            ids_high = jnp.floor(ids * (1.0 / 32.0))
            ids_low = ids - 32.0 * ids_high
            wide = 32.0 * product(ids_high.astype(BF16), spread) + product(ids_low.astype(BF16), spread)
            flat = jnp.sum(jnp.where(own_lane, wide, 0.0), axis=0, keepdims=True).astype(jnp.int32) - 1
            places.append(onehot(iota((CELLS, group), 0) == flat))
        high, low = halves(got_rows[pl.ds(turn * ny, 2 * ny)].reshape(2 * group, CY))
        total[...] += product(jnp.concatenate(places, axis=1), jnp.concatenate([high, low], axis=1))
        return carry

    lax.fori_loop(0, nx // 2, lambda pair, carry: collect(2 * pair, carry), 0)

    def strain(i, carry):
        at = pl.ds(2 * i * NZ, 2 * NZ)
        for odd, slab in enumerate(slabs_of(total[at, :CY] + total[at, CY:], 0)):
            x = 2 * i + odd
            slab = stress[x + 1] * slab
            stress[x + 1] = slab
            slice_up(slab, x + 1)
            store_ends(slab, x, packed_stress)
        return carry

    lax.fori_loop(0, CX // 2, strain, 0)
    over(stress_faces, start)
    over(stress_sides, start)
    at = pl.ds(1, CX)
    differed[at] = product(sliced[at].reshape(CX * NZ, 2 * CY), along_matrix[:, CY:]).reshape((CX,) + SLAB)
    over(from_stress_sides, receive)
    for g in range(2):
        ends[0, pl.ds(g * ROWS, ROWS)] = merge_ends(got_stress_ends[0, g], got_stress_ends[1, g])
    over(from_stress_faces, receive)

    def keep_moved(sweep, x, c, moved, step):
        at = x + 1
        steps[c, x] = step
        fields[sweep + 1, c, at] = moved
        slice_up(moved, c * SLABS + at)
        store_ends(moved, x, packed.at[sweep + 1, c])

    def softer(sweep, x):
        return jnp.where(born[x] <= sweep, 1.0, 1.0 / SOFTENED)

    first_gain = 1.0 / theta

    def first_move(x):
        middle = stress[x + 1]
        scale = 0.5 * inverse[x]
        soft = softer(0, x)
        added = ends[0, pl.ds(x, 1), :]
        gradients = (differed[x + 1], stress[x + 2] - stress[x], up(middle, added) - down(middle, added))
        for c, gradient in enumerate(gradients):
            force = scale * gradient
            forces[c, x] = force
            step = first_gain * (steps[c, x] + soft * force)
            keep_moved(0, x, c, fields[0, c, x + 1] + step, step)

    def ends_first(move, sweep):
        lax.fori_loop(0, 2, lambda i, carry: (move(i * (CX - 1)), carry)[1], 0, unroll=2)
        over(faces(sweep + 1), start)
        lax.fori_loop(1, CX - 1, lambda x, carry: (move(x), carry)[1], 0, unroll=2)
        over(edges(sweep + 1), start)
        along_own(sweep + 1)

    ends_first(first_move, 0)

    for sweep in range(1, SWEEPS):
        ratio_next = 1.0 / (2.0 * sigma - ratio)
        keep = ratio_next * ratio
        gain = 2.0 * ratio_next / delta
        ratio = ratio_next
        along_halo(sweep)

        def moves(x, sweep=sweep, keep=keep, gain=gain):
            soft = softer(sweep, x)
            for c in range(3):
                step = gain * (rest(sweep, x, c) + soft * forces[c, x]) + keep * steps[c, x]
                yield c, fields[sweep, c, x + 1] + step, step

        if sweep < SWEEPS - 1:

            def move(x, sweep=sweep, moves=moves):
                for c, moved, step in moves(x):
                    keep_moved(sweep, x, c, moved, step)

            ends_first(move, sweep)
        else:

            def last(i, carry, moves=moves):
                both = [[moved for _, moved, _ in moves(2 * i + odd)] for odd in range(2)]
                for c in range(3):
                    block = pair_of_slabs([both[0][c], both[1][c]], c)
                    for odd in range(2):
                        for part in range(NZ // ROWS):
                            first = odd * NZ + part * ROWS
                            out_ref[c, rows_of(2 * i + odd, part), :] = block[first : first + ROWS]
                return carry

            lax.fori_loop(0, CX // 2, last, 0)

    pltpu.make_async_copy(column_ids.at[from_column], column_ids.at[from_column], column_send_sem).wait()
    pltpu.make_async_copy(got_ids.at[:, from_line], got_ids.at[:, from_line], ids_send_sem).wait()
    pltpu.make_async_copy(send_rows.at[others], send_rows.at[others], rows_send_sem).wait()
    over(stress_faces + stress_sides, finish)
    for sweep in range(SWEEPS):
        over(edges(sweep) + faces(sweep), finish)


def local(thermal_rows, row_owner, row_element, modulus, birth, start_disp, bounds):
    nx, ny = lax.axis_size("gx"), lax.axis_size("gy")
    tiles = nx * ny
    count = thermal_rows.shape[0]
    vmem, dma = pltpu.VMEM, pltpu.SemaphoreType.DMA
    moved = pl.pallas_call(
        functools.partial(kernel, nx, ny),
        out_shape=jax.ShapeDtypeStruct((3, CELLS, CY), F32),
        in_specs=[pl.BlockSpec(memory_space=pltpu.HBM)] * 6 + [pl.BlockSpec(memory_space=pltpu.SMEM)],
        out_specs=pl.BlockSpec(memory_space=pltpu.VMEM),
        scratch_shapes=[
            vmem((1, count), jnp.int32),
            vmem((1, count), jnp.int32),
            vmem((count, CY), F32),
            vmem((CELLS, CY), F32),
            vmem((CELLS, CY), jnp.int32),
            vmem((3, CELLS, CY), F32),
            dma((6,)),
            vmem((count, 2 * CY), BF16),
            vmem((1, count), jnp.int32),
            vmem((tiles, CAP, CY), F32),
            vmem((nx, ny, 1, CY), F32),
            vmem((nx, ny, 1, CY), F32),
            vmem((tiles, CAP, CY), F32),
            vmem((nx, ny, 1, CY), F32),
            vmem((CELLS, 2 * CY), F32),
            pltpu.SemaphoreType.REGULAR,
            dma, dma, dma, dma, dma, dma((nx,)),
            vmem((SWEEPS, 3, SLABS) + SLAB, F32),
            vmem((SLABS,) + SLAB, F32),
            vmem((CX,) + SLAB, F32),
            vmem((3, CX) + SLAB, F32),
            vmem((CX,) + SLAB, F32),
            vmem((3, CX) + SLAB, F32),
            vmem((3 * SLABS,) + SLAB, F32),
            vmem((3 * SLABS,) + SLAB, F32),
            vmem((3 * SLABS, NZ, 2 * CY), BF16),
            vmem((2 * CY, 2 * CY), BF16),
            vmem((6, NZ, CY), F32),
            vmem((SWEEPS, 3, 2, ROWS, CY), F32),
            vmem((2, ROWS, CY), F32),
            vmem((SWEEPS, 2, 3, 4, ROWS, CY), F32),
            vmem((2, 2, ROWS, CY), F32),
            vmem((3, 4 * ROWS, CY), F32),
            vmem((3, 4 * ROWS, CY), F32),
            vmem((3, 4 * ROWS, CY), F32),
            vmem((3, CX, CY), F32),
            dma((SWEEPS, 2)), dma((SWEEPS, 2)), dma((SWEEPS, 2)), dma((SWEEPS, 2)), dma((SWEEPS, 4)), dma((SWEEPS, 4)),
            dma((2,)), dma((2,)), dma((2,)), dma((2,)),
        ],
        compiler_params=pltpu.CompilerParams(
            collective_id=0, has_side_effects=True, vmem_limit_bytes=60 * 1024 * 1024
        ),
        name="weld",
    )(
        row_owner.reshape(1, count), row_element.reshape(1, count), thermal_rows,
        modulus.reshape(CELLS, CY), birth.reshape(CELLS, CY), start_disp.reshape(3, CELLS, CY), bounds,
    )
    return moved.reshape(start_disp.shape)


def solution(mesh):
    placed = (
        P(("gx", "gy"), None),
        P(("gx", "gy"), None),
        P(("gx", "gy"), None),
        P(None, "gx", "gy"),
        P(None, "gx", "gy"),
        P(None, None, "gx", "gy"),
        P(),
    )
    return jax.shard_map(
        local, mesh=mesh, in_specs=placed, out_specs=P(None, None, "gx", "gy"), check_vma=False
    )
```

```python
import functools

import jax
import jax.numpy as jnp
from jax import lax
from jax.experimental import pallas as pl
from jax.experimental.pallas import tpu as pltpu
from jax.sharding import PartitionSpec as P

SWEEPS = 4
CAP = 24
TOGETHER = 4
FIRST = 2
SECOND = 4
NZ = 64
CX = 16
CY = 128
ROWS = 8
PARTS = 8
HALF = CY // 2
CELLS = NZ * CX
SLABS = CX + 2
SLAB = (PARTS, ROWS, CY)
DIAGONAL_WEIGHT = 14.5
COUPLING = 0.25
SOFTENED = 0.05

MESH = pl.DeviceIdType.MESH
F32 = jnp.float32
BF16 = jnp.bfloat16


def halves(values):
    high = values.astype(BF16)
    low = (values - high.astype(F32)).astype(BF16)
    return high, low


def onehot(matches):
    return jnp.where(matches, 1.0, 0.0).astype(BF16)


def iota(shape, dim):
    return lax.broadcasted_iota(jnp.int32, shape, dim)


def product(left, right):
    return jnp.dot(left, right, preferred_element_type=F32)


def row_index():
    return iota((ROWS, CY), 0)


def in_first_half():
    return iota((ROWS, CY), 1) < HALF


def up(slab, ends):
    first = pltpu.roll(slab[0], ROWS - 1, 0)
    turned = jnp.where(in_first_half(), pltpu.roll(first, HALF, 1), ends)
    return jnp.concatenate([slab[1:], jnp.where(row_index() == ROWS - 1, turned, first)[None]], axis=0)


def down(slab, ends):
    last = pltpu.roll(slab[PARTS - 1], 1, 0)
    turned = jnp.where(in_first_half(), ends, pltpu.roll(last, HALF, 1))
    return jnp.concatenate([jnp.where(row_index() == 0, turned, last)[None], slab[:-1]], axis=0)


def end_row(slab):
    return jnp.where(iota((1, CY), 1) < HALF, slab[0][:1], pltpu.roll(slab[PARTS - 1], 1, 0)[:1])


def turn_halves(values):
    return pltpu.roll(values, HALF, 1)


def kernel(
    nx, ny,
    owner_hbm, element_hbm, rows_hbm, modulus_hbm, birth_hbm, start_hbm, bounds_ref,
    out_ref,
    owner_ref, element_ref, rows_ref, modulus_ref, birth_ref, start_ref, in_sem,
    split_ref, place_ref, send_rows, send_ids, column_ids, got_rows, got_ids, total,
    ready_sem, column_send_sem, column_recv_sem, ids_send_sem, ids_recv_sem, rows_send_sem, rows_recv_sem,
    fields, stress, inverse, forces, born, steps, summed, differed, sliced,
    along_matrix, turning,
    packed, corner_rows, packed_stress, got_ends, got_stress_ends, ends, ends_summed, ends_differed, ends_added,
    face_send, face_recv, side_send, side_recv, corner_send, corner_recv,
    stress_face_send, stress_face_recv, stress_side_send, stress_side_recv,
):
    tiles = nx * ny
    count = rows_ref.shape[0]
    group = ny * CAP
    gx = lax.axis_index("gx")
    gy = lax.axis_index("gy")

    loads = [
        pltpu.make_async_copy(source, target, in_sem.at[i])
        for i, (source, target) in enumerate(
            [
                (owner_hbm, owner_ref), (element_hbm, element_ref), (rows_hbm, rows_ref),
                (start_hbm, start_ref), (modulus_hbm, modulus_ref), (birth_hbm, birth_ref),
            ]
        )
    ]
    for load in loads:
        load.start()

    def in_column(turn):
        return lax.rem(gx + turn, nx), gy

    def in_line(turn):
        return gx, lax.rem(gy + turn, ny)

    barrier = pltpu.get_barrier_semaphore()

    def greet_line(turn, carry):
        pl.semaphore_signal(barrier, inc=1, device_id=in_line(turn), device_id_type=MESH)
        return carry

    def greet_column(turn, carry):
        pl.semaphore_signal(barrier, inc=1, device_id=in_column(turn), device_id_type=MESH)
        return carry

    def tell_column(turn, carry):
        pl.semaphore_signal(ready_sem, inc=1, device_id=in_column(turn), device_id_type=MESH)
        return carry

    lax.fori_loop(1, ny, greet_line, 0)
    lax.fori_loop(1, nx, greet_column, 0)

    has = {-1: (gx > 0, gy > 0), 1: (gx < nx - 1, gy < ny - 1)}

    def present(a, b):
        if a == 0:
            return has[b][1]
        if b == 0:
            return has[a][0]
        return jnp.logical_and(has[a][0], has[b][1])

    def over(copies, do):
        for where, copy in copies:

            @pl.when(present(*where))
            def _(copy=copy):
                do(copy())

    loads[0].wait()
    loads[1].wait()
    owner = owner_ref[...]
    given = element_ref[...]
    depth_index = given // CX
    element = lax.rem(given, CX) * NZ + depth_index + 1
    member = jnp.where(iota((tiles, count), 0) == owner, 1.0, 0.0)
    member16 = member.astype(BF16)
    block = 256
    earlier = onehot(iota((block, block), 0) < iota((block, block), 1))
    carried = jnp.zeros((tiles, 1), F32)
    slots = []
    for first in range(0, count, block):
        part = member[:, first : first + block]
        before = product(member16[:, first : first + block], earlier) + carried
        slots.append(jnp.sum(before * part, axis=0, keepdims=True))
        carried = carried + jnp.sum(part, axis=1, keepdims=True)
    slot = jnp.concatenate(slots, axis=1).astype(jnp.int32)
    place_ref[...] = owner * CAP + slot

    pl.semaphore_wait(barrier, nx + ny - 2)
    lax.fori_loop(1, nx, tell_column, 0)

    loads[2].wait()
    high, low = halves(rows_ref[...])
    split_ref[:, :CY] = high
    split_ref[:, CY:] = low

    pl.semaphore_wait(ready_sem, nx - 1)

    def pack_rows(turn, carry):
        tile_x = lax.rem(gx + turn, nx)
        wanted = tile_x * group + iota((group, count), 0)
        picked = product(onehot(wanted == place_ref[...]), split_ref[...])
        send_rows[pl.ds(tile_x * ny, ny)] = (picked[:, :CY] + picked[:, CY:]).reshape(ny, CAP, CY)

        def send(turn_y, carry):
            tile_y = lax.rem(gy + turn_y, ny)
            pltpu.make_async_remote_copy(
                src_ref=send_rows.at[tile_x * ny + tile_y], dst_ref=got_rows.at[turn * ny + turn_y],
                send_sem=rows_send_sem, recv_sem=rows_recv_sem.at[turn],
                device_id=(tile_x, tile_y), device_id_type=MESH,
            ).start()
            return carry

        @pl.when(turn == 0)
        def _():
            lax.fori_loop(1, ny, send, 0)

        @pl.when(turn > 0)
        def _():
            lax.fori_loop(0, ny, send, 0)

        return carry

    lax.fori_loop(0, FIRST, pack_rows, 0)

    weighed = jnp.concatenate(
        [
            (member * (element // 32).astype(F32)).astype(BF16),
            (member * lax.rem(element, 32).astype(F32)).astype(BF16),
        ],
        axis=0,
    )
    slot_of = onehot(iota((CY, count), 0) == slot)
    both = lax.dot_general(weighed, slot_of, (((1,), (1,)), ((), ())), preferred_element_type=F32)
    send_ids[...] = (32.0 * both[:tiles] + both[tiles:]).reshape(nx, ny, 1, CY)

    def send_ids_down(turn, carry):
        to = in_column(turn)
        pltpu.make_async_remote_copy(
            src_ref=send_ids.at[to[0]], dst_ref=column_ids.at[turn],
            send_sem=column_send_sem, recv_sem=column_recv_sem,
            device_id=to, device_id_type=MESH,
        ).start()
        return carry

    lax.fori_loop(1, nx, send_ids_down, 0)
    column_ids[0] = send_ids[gx]

    def send_ids_along(turn, carry):
        to = in_line(turn)
        pltpu.make_async_remote_copy(
            src_ref=column_ids.at[:, to[1]], dst_ref=got_ids.at[:, turn],
            send_sem=ids_send_sem, recv_sem=ids_recv_sem,
            device_id=to, device_id_type=MESH,
        ).start()
        return carry

    zeros = jnp.zeros((ROWS, CY), F32)
    corner_rows[...] = jnp.zeros_like(corner_rows)
    for hand, slab_at, group_at in ((-1, 0, 0), (1, CX + 1, 3)):

        @pl.when(jnp.logical_not(has[hand][0]))
        def _(slab_at=slab_at, group_at=group_at):
            stress[slab_at] = jnp.zeros(SLAB, F32)
            for sweep in range(SWEEPS):
                for c in range(3):
                    fields[sweep, c, slab_at] = jnp.zeros(SLAB, F32)
                    for side_at in range(2):
                        got_ends[sweep, side_at, c, group_at] = zeros

        @pl.when(jnp.logical_not(has[hand][1]))
        def _(side_at=(hand + 1) // 2):
            got_stress_ends[side_at] = jnp.zeros((2, ROWS, CY), F32)
            for sweep in range(SWEEPS):
                for c in range(3):
                    got_ends[sweep, side_at, c] = jnp.zeros((4, ROWS, CY), F32)

    row, column = iota((2 * CY, 2 * CY), 0), iota((2 * CY, 2 * CY), 1)
    k, z = lax.rem(row, CY), lax.rem(column, CY)
    off = jnp.where(k // NZ == z // NZ, k - z, 2)
    after, before = jnp.where(off == 1, 1.0, 0.0), jnp.where(off == -1, 1.0, 0.0)
    sums = jnp.where(off == 0, 2.0, after + before)
    along_matrix[...] = jnp.where(column < CY, sums, after - before).astype(BF16)

    first_half = iota((2 * NZ // 2, CY), 1) < HALF

    def slabs_of(pair, at):
        turned = pair.T
        begin, end = turned[:NZ], turned[NZ:]
        slabs = []
        for odd, values in enumerate(
            (jnp.where(first_half, begin, turn_halves(end)), jnp.where(first_half, turn_halves(begin), end))
        ):
            turning[2 * at + odd] = values
            slabs.append(jnp.stack([turning[2 * at + odd, pl.ds(part, ROWS, stride=PARTS), :] for part in range(PARTS)]))
        return slabs

    def pair_of_slabs(slabs, at):
        for odd in range(2):
            for part in range(PARTS):
                turning[2 * at + odd, pl.ds(part, ROWS, stride=PARTS), :] = slabs[odd][part]
        even, odd = turning[2 * at], turning[2 * at + 1]
        return jnp.concatenate(
            [jnp.where(first_half, even, turn_halves(odd)), jnp.where(first_half, turn_halves(even), odd)], axis=0
        ).T

    def over_pairs(body):
        def some(i, carry):
            for at in range(TOGETHER):
                body(TOGETHER * i + at, 3 * at)
            return carry

        lax.fori_loop(0, CX // 2 // TOGETHER, some, 0)

    def rows_of(x, part):
        return pl.ds(part * ROWS * CX + x, ROWS, stride=CX)

    def take(ref, i):
        return jnp.concatenate([ref[rows_of(2 * i + odd, part), :] for odd in range(2) for part in range(NZ // ROWS)], axis=0)

    def slice_up(slab, at):
        high, low = halves(slab.reshape(NZ, CY))
        sliced[at, :, :CY] = high
        sliced[at, :, CY:] = low

    def merge_ends(from_left, from_right):
        return turn_halves(jnp.where(in_first_half(), from_right, from_left))

    def face(sweep, a):
        mine, theirs = (1, CX + 1) if a < 0 else (CX, 0)
        return pltpu.make_async_remote_copy(
            src_ref=fields.at[sweep, :, mine], dst_ref=fields.at[sweep, :, theirs],
            send_sem=face_send.at[sweep, (a + 1) // 2], recv_sem=face_recv.at[sweep, (1 - a) // 2],
            device_id=(gx + a, gy), device_id_type=MESH,
        )

    def side(sweep, b):
        return pltpu.make_async_remote_copy(
            src_ref=packed.at[sweep], dst_ref=got_ends.at[sweep, (1 - b) // 2, :, pl.ds(1, 2)],
            send_sem=side_send.at[sweep, (b + 1) // 2], recv_sem=side_recv.at[sweep, (1 - b) // 2],
            device_id=(gx, gy + b), device_id_type=MESH,
        )

    def corner(sweep, a, b):
        mine, theirs = (0, 3) if a < 0 else (1, 0)
        return pltpu.make_async_remote_copy(
            src_ref=corner_rows.at[sweep, :, mine], dst_ref=got_ends.at[sweep, (1 - b) // 2, :, theirs],
            send_sem=corner_send.at[sweep, a + 1 + (b + 1) // 2], recv_sem=corner_recv.at[sweep, 1 - a + (1 - b) // 2],
            device_id=(gx + a, gy + b), device_id_type=MESH,
        )

    def stress_face(a):
        mine, theirs = (1, CX + 1) if a < 0 else (CX, 0)
        return pltpu.make_async_remote_copy(
            src_ref=stress.at[mine], dst_ref=stress.at[theirs],
            send_sem=stress_face_send.at[(a + 1) // 2], recv_sem=stress_face_recv.at[(1 - a) // 2],
            device_id=(gx + a, gy), device_id_type=MESH,
        )

    def stress_side(b):
        return pltpu.make_async_remote_copy(
            src_ref=packed_stress, dst_ref=got_stress_ends.at[(1 - b) // 2],
            send_sem=stress_side_send.at[(b + 1) // 2], recv_sem=stress_side_recv.at[(1 - b) // 2],
            device_id=(gx, gy + b), device_id_type=MESH,
        )

    pair_of = (-1, 1)

    def faces(sweep):
        return [((a, 0), lambda a=a: face(sweep, a)) for a in pair_of]

    def sides(sweep):
        return [((0, b), lambda b=b: side(sweep, b)) for b in pair_of]

    def corners(sweep):
        return [((a, b), lambda a=a, b=b: corner(sweep, a, b)) for a in pair_of for b in pair_of]

    stress_faces = [((a, 0), lambda a=a: stress_face(a)) for a in pair_of]
    stress_sides = [((0, b), lambda b=b: stress_side(b)) for b in pair_of]

    def arrival(ref, sem):
        return lambda: pltpu.make_async_copy(ref, ref, sem)

    def from_faces(sweep):
        return [
            ((a, 0), arrival(fields.at[sweep, :, 0 if a < 0 else CX + 1], face_recv.at[sweep, (a + 1) // 2]))
            for a in pair_of
        ]

    def from_edges(sweep):
        return [
            ((0, b), arrival(got_ends.at[sweep, (b + 1) // 2, :, pl.ds(1, 2)], side_recv.at[sweep, (b + 1) // 2]))
            for b in pair_of
        ] + [
            (
                (a, b),
                arrival(
                    got_ends.at[sweep, (b + 1) // 2, :, 0 if a < 0 else 3],
                    corner_recv.at[sweep, a + 1 + (b + 1) // 2],
                ),
            )
            for a in pair_of
            for b in pair_of
        ]

    from_stress_faces = [
        ((a, 0), arrival(stress.at[0 if a < 0 else CX + 1], stress_face_recv.at[(a + 1) // 2])) for a in pair_of
    ]
    from_stress_sides = [
        ((0, b), arrival(got_stress_ends.at[(b + 1) // 2], stress_side_recv.at[(b + 1) // 2])) for b in pair_of
    ]

    def start(copy):
        copy.start()

    def receive(copy):
        copy.wait()

    def finish(copy):
        copy.wait_send()

    def along_own(sweep):
        for c in range(3):
            at = pl.ds(c * SLABS + 1, CX)
            both = product(sliced[at].reshape(CX * NZ, 2 * CY), along_matrix[...])
            summed[at] = both[:, :CY].reshape((CX,) + SLAB)
            differed[at] = both[:, CY:].reshape((CX,) + SLAB)

    def along_halo(sweep):
        over(from_edges(sweep) + from_faces(sweep), receive)
        for c in range(3):
            for g in range(4):
                at = pl.ds(g * ROWS, ROWS)
                ends[c, at] = merge_ends(got_ends[sweep, 0, c, g], got_ends[sweep, 1, c, g])
        halo = [fields[sweep, c, at].reshape(NZ, CY) for c in range(3) for at in (0, CX + 1)]
        high, low = halves(jnp.concatenate(halo + [ends[c] for c in range(3)], axis=0))
        both = product(jnp.concatenate([high, low], axis=1), along_matrix[...])
        for c in range(3):
            for hand, at in enumerate((0, CX + 1)):
                first = (2 * c + hand) * NZ
                summed[c * SLABS + at] = both[first : first + NZ, :CY].reshape(SLAB)
                differed[c * SLABS + at] = both[first : first + NZ, CY:].reshape(SLAB)
            first = 6 * NZ + c * 4 * ROWS
            ends_summed[c] = both[first : first + 4 * ROWS, :CY]
            ends_differed[c] = both[first : first + 4 * ROWS, CY:]

        def near(ref, c, step):
            return ref[c, pl.ds(ROWS + step, CX), :]

        for c in range(3):
            around = (near(ends_summed, c, -1) + near(ends_summed, c, 1)) + 2.0 * near(ends_summed, c, 0)
            if c == 0:
                across = near(ends_differed, 2, 0)
            elif c == 1:
                across = near(ends, 2, 1) - near(ends, 2, -1)
            else:
                across = near(ends_differed, 0, 0) + (near(ends, 1, 1) - near(ends, 1, -1))
            sign = jnp.where(iota((CX, CY), 1) < HALF, -COUPLING, COUPLING)
            ends_added[c] = around + sign * across

    def rest(sweep, x, c):
        at = x + 1

        def field(component, to):
            return fields[sweep, component, to]

        def along_sum(to):
            return summed[c * SLABS + to]

        def along_difference(component, to):
            return differed[component * SLABS + to]

        around = (along_sum(at - 1) + along_sum(at + 1)) + 2.0 * along_sum(at)
        if c == 0:
            across = along_difference(2, at)
        elif c == 1:
            across = field(2, at + 1) - field(2, at - 1)
        else:
            across = along_difference(0, at) + (field(1, at + 1) - field(1, at - 1))
        across = COUPLING * across
        added = ends_added[c, pl.ds(x, 1), :]
        total_around = (up(around + across, added) + down(around - across, added)) + 2.0 * around
        if c < 2:
            total_around = total_around + COUPLING * (along_difference(1 - c, at + 1) - along_difference(1 - c, at - 1))
        return (0.25 / DIAGONAL_WEIGHT) * total_around - ((DIAGONAL_WEIGHT + 2.0) / DIAGONAL_WEIGHT) * field(c, at)

    loads[3].wait()

    def store_ends(slab, x, ref):
        ref[x // ROWS, pl.ds(lax.rem(x, ROWS), 1), :] = end_row(slab)

    def keep_corners(sweep, which):
        row = pl.ds((ROWS - 1) * which, 1)
        for c in range(3):
            corner_rows[sweep, c, which, row, :] = packed[sweep, c, which, row, :]

    def begin(i, room):
        for c in range(3):
            for odd, slab in enumerate(slabs_of(take(start_ref.at[c], i), room + c)):
                x = 2 * i + odd
                fields[0, c, x + 1] = slab
                slice_up(slab, c * SLABS + x + 1)
                store_ends(slab, x, packed.at[0, c])

    over_pairs(begin)
    for which in range(2):
        keep_corners(0, which)
    over(corners(0) + sides(0) + faces(0), start)
    lax.fori_loop(FIRST, SECOND, pack_rows, 0)
    from_column = pl.ds(1, nx - 1)
    pltpu.make_async_copy(column_ids.at[from_column], column_ids.at[from_column], column_recv_sem).wait()
    lax.fori_loop(1, ny, send_ids_along, 0)
    got_ids[:, 0] = column_ids[:, gy]
    lax.fori_loop(SECOND, nx, pack_rows, 0)
    got_rows[0] = send_rows[gx * ny + gy]

    loads[4].wait()
    loads[5].wait()

    def material(i, room):
        for odd, modulus in enumerate(slabs_of(take(modulus_ref, i), room)):
            x = 2 * i + odd
            stress[x + 1] = modulus
            inverse[x] = 1.0 / (DIAGONAL_WEIGHT * modulus)
        for odd, birth in enumerate(slabs_of(take(birth_ref, i).astype(F32), room + 1)):
            born[2 * i + odd] = birth

    over_pairs(material)
    along_own(0)

    lower = jnp.full((ROWS, CY), bounds_ref[0], F32)
    upper = jnp.full((ROWS, CY), bounds_ref[1], F32)
    theta = (upper + lower) / 2.0
    delta = (upper - lower) / 2.0
    sigma = theta / delta
    ratio = 1.0 / sigma

    along_halo(0)

    def first_rest(x, carry):
        for c in range(3):
            steps[c, x] = rest(0, x, c)
        return carry

    lax.fori_loop(0, CX, first_rest, 0, unroll=2)

    others = pl.ds(1, tiles - 1)
    from_line = pl.ds(1, ny - 1)
    pltpu.make_async_copy(got_ids.at[:, from_line], got_ids.at[:, from_line], ids_recv_sem).wait()
    spread = onehot(iota((CY, group), 0) == lax.rem(iota((CY, group), 1), CAP))
    own_lane = iota((ny, group), 0) == iota((ny, group), 1) // CAP
    total[...] = jnp.zeros_like(total)

    def collect(turn, carry):
        @pl.when(turn == 0)
        def _():
            part = got_rows.at[pl.ds(1, ny - 1)]
            pltpu.make_async_copy(part, part, rows_recv_sem.at[0]).wait()

        @pl.when(turn > 0)
        def _():
            part = got_rows.at[pl.ds(turn * ny, ny)]
            pltpu.make_async_copy(part, part, rows_recv_sem.at[turn]).wait()

        part = got_rows.at[pl.ds((turn + 1) * ny, ny)]
        pltpu.make_async_copy(part, part, rows_recv_sem.at[turn + 1]).wait()
        places = []
        for at in range(2):
            ids = got_ids[turn + at].reshape(ny, CY)
            ids_high = jnp.floor(ids * (1.0 / 32.0))
            ids_low = ids - 32.0 * ids_high
            wide = 32.0 * product(ids_high.astype(BF16), spread) + product(ids_low.astype(BF16), spread)
            flat = jnp.sum(jnp.where(own_lane, wide, 0.0), axis=0, keepdims=True).astype(jnp.int32) - 1
            places.append(onehot(iota((CELLS, group), 0) == flat))
        high, low = halves(got_rows[pl.ds(turn * ny, 2 * ny)].reshape(2 * group, CY))
        total[...] += product(jnp.concatenate(places, axis=1), jnp.concatenate([high, low], axis=1))
        return carry

    lax.fori_loop(0, nx // 2, lambda pair, carry: collect(2 * pair, carry), 0)

    def strain(i, room):
        at = pl.ds(2 * i * NZ, 2 * NZ)
        for odd, slab in enumerate(slabs_of(total[at, :CY] + total[at, CY:], room)):
            x = 2 * i + odd
            slab = stress[x + 1] * slab
            stress[x + 1] = slab
            slice_up(slab, x + 1)
            store_ends(slab, x, packed_stress)

    over_pairs(strain)
    over(stress_faces, start)
    over(stress_sides, start)
    at = pl.ds(1, CX)
    differed[at] = product(sliced[at].reshape(CX * NZ, 2 * CY), along_matrix[:, CY:]).reshape((CX,) + SLAB)
    over(from_stress_sides, receive)
    for g in range(2):
        ends[0, pl.ds(g * ROWS, ROWS)] = merge_ends(got_stress_ends[0, g], got_stress_ends[1, g])
    over(from_stress_faces, receive)

    def keep_moved(sweep, x, c, moved, step):
        at = x + 1
        steps[c, x] = step
        fields[sweep + 1, c, at] = moved
        slice_up(moved, c * SLABS + at)
        store_ends(moved, x, packed.at[sweep + 1, c])

    def softer(sweep, x):
        return jnp.where(born[x] <= sweep, 1.0, 1.0 / SOFTENED)

    first_gain = 1.0 / theta

    def first_move(x):
        middle = stress[x + 1]
        scale = 0.5 * inverse[x]
        soft = softer(0, x)
        added = ends[0, pl.ds(x, 1), :]
        gradients = (differed[x + 1], stress[x + 2] - stress[x], up(middle, added) - down(middle, added))
        for c, gradient in enumerate(gradients):
            force = scale * gradient
            forces[c, x] = force
            step = first_gain * (steps[c, x] + soft * force)
            keep_moved(0, x, c, fields[0, c, x + 1] + step, step)

    def ends_first(move, sweep):
        lax.fori_loop(0, 2, lambda i, carry: (move(i * (CX - 1)), carry)[1], 0, unroll=2)
        for which in range(2):
            keep_corners(sweep + 1, which)
        over(corners(sweep + 1) + faces(sweep + 1), start)
        lax.fori_loop(1, CX - 1, lambda x, carry: (move(x), carry)[1], 0, unroll=2)
        over(sides(sweep + 1), start)
        along_own(sweep + 1)

    ends_first(first_move, 0)

    for sweep in range(1, SWEEPS):
        ratio_next = 1.0 / (2.0 * sigma - ratio)
        keep = ratio_next * ratio
        gain = 2.0 * ratio_next / delta
        ratio = ratio_next
        along_halo(sweep)

        def moves(x, sweep=sweep, keep=keep, gain=gain):
            soft = softer(sweep, x)
            for c in range(3):
                step = gain * (rest(sweep, x, c) + soft * forces[c, x]) + keep * steps[c, x]
                yield c, fields[sweep, c, x + 1] + step, step

        if sweep < SWEEPS - 1:

            def move(x, sweep=sweep, moves=moves):
                for c, moved, step in moves(x):
                    keep_moved(sweep, x, c, moved, step)

            ends_first(move, sweep)
        else:

            def last(i, room, moves=moves):
                both = [[moved for _, moved, _ in moves(2 * i + odd)] for odd in range(2)]
                for c in range(3):
                    block = pair_of_slabs([both[0][c], both[1][c]], room + c)
                    for odd in range(2):
                        for part in range(NZ // ROWS):
                            first = odd * NZ + part * ROWS
                            out_ref[c, rows_of(2 * i + odd, part), :] = block[first : first + ROWS]

            over_pairs(last)

    pltpu.make_async_copy(column_ids.at[from_column], column_ids.at[from_column], column_send_sem).wait()
    pltpu.make_async_copy(got_ids.at[:, from_line], got_ids.at[:, from_line], ids_send_sem).wait()
    pltpu.make_async_copy(send_rows.at[others], send_rows.at[others], rows_send_sem).wait()
    over(stress_faces + stress_sides, finish)
    for sweep in range(SWEEPS):
        over(corners(sweep) + sides(sweep) + faces(sweep), finish)


def local(thermal_rows, row_owner, row_element, modulus, birth, start_disp, bounds):
    nx, ny = lax.axis_size("gx"), lax.axis_size("gy")
    tiles = nx * ny
    count = thermal_rows.shape[0]
    vmem, dma = pltpu.VMEM, pltpu.SemaphoreType.DMA
    moved = pl.pallas_call(
        functools.partial(kernel, nx, ny),
        out_shape=jax.ShapeDtypeStruct((3, CELLS, CY), F32),
        in_specs=[pl.BlockSpec(memory_space=pltpu.HBM)] * 6 + [pl.BlockSpec(memory_space=pltpu.SMEM)],
        out_specs=pl.BlockSpec(memory_space=pltpu.VMEM),
        scratch_shapes=[
            vmem((1, count), jnp.int32),
            vmem((1, count), jnp.int32),
            vmem((count, CY), F32),
            vmem((CELLS, CY), F32),
            vmem((CELLS, CY), jnp.int32),
            vmem((3, CELLS, CY), F32),
            dma((6,)),
            vmem((count, 2 * CY), BF16),
            vmem((1, count), jnp.int32),
            vmem((tiles, CAP, CY), F32),
            vmem((nx, ny, 1, CY), F32),
            vmem((nx, ny, 1, CY), F32),
            vmem((tiles, CAP, CY), F32),
            vmem((nx, ny, 1, CY), F32),
            vmem((CELLS, 2 * CY), F32),
            pltpu.SemaphoreType.REGULAR,
            dma, dma, dma, dma, dma, dma((nx,)),
            vmem((SWEEPS, 3, SLABS) + SLAB, F32),
            vmem((SLABS,) + SLAB, F32),
            vmem((CX,) + SLAB, F32),
            vmem((3, CX) + SLAB, F32),
            vmem((CX,) + SLAB, F32),
            vmem((3, CX) + SLAB, F32),
            vmem((3 * SLABS,) + SLAB, F32),
            vmem((3 * SLABS,) + SLAB, F32),
            vmem((3 * SLABS, NZ, 2 * CY), BF16),
            vmem((2 * CY, 2 * CY), BF16),
            vmem((6 * TOGETHER, NZ, CY), F32),
            vmem((SWEEPS, 3, 2, ROWS, CY), F32),
            vmem((SWEEPS, 3, 2, ROWS, CY), F32),
            vmem((2, ROWS, CY), F32),
            vmem((SWEEPS, 2, 3, 4, ROWS, CY), F32),
            vmem((2, 2, ROWS, CY), F32),
            vmem((3, 4 * ROWS, CY), F32),
            vmem((3, 4 * ROWS, CY), F32),
            vmem((3, 4 * ROWS, CY), F32),
            vmem((3, CX, CY), F32),
            dma((SWEEPS, 2)), dma((SWEEPS, 2)), dma((SWEEPS, 2)), dma((SWEEPS, 2)), dma((SWEEPS, 4)), dma((SWEEPS, 4)),
            dma((2,)), dma((2,)), dma((2,)), dma((2,)),
        ],
        compiler_params=pltpu.CompilerParams(
            collective_id=0, has_side_effects=True, vmem_limit_bytes=60 * 1024 * 1024
        ),
        name="weld",
    )(
        row_owner.reshape(1, count), row_element.reshape(1, count), thermal_rows,
        modulus.reshape(CELLS, CY), birth.reshape(CELLS, CY), start_disp.reshape(3, CELLS, CY), bounds,
    )
    return moved.reshape(start_disp.shape)


def solution(mesh):
    placed = (
        P(("gx", "gy"), None),
        P(("gx", "gy"), None),
        P(("gx", "gy"), None),
        P(None, "gx", "gy"),
        P(None, "gx", "gy"),
        P(None, None, "gx", "gy"),
        P(),
    )
    return jax.shard_map(
        local, mesh=mesh, in_specs=placed, out_specs=P(None, None, "gx", "gy"), check_vma=False
    )
```

```python
import functools

import jax
import jax.numpy as jnp
from jax import lax
from jax.experimental import pallas as pl
from jax.experimental.pallas import tpu as pltpu
from jax.sharding import PartitionSpec as P

SWEEPS = 4
CAP = 24
TOGETHER = 8
FIRST = 2
SECOND = 4
NZ = 64
CX = 16
CY = 128
ROWS = 8
PARTS = 8
HALF = CY // 2
CELLS = NZ * CX
SLABS = CX + 2
SLAB = (PARTS, ROWS, CY)
DIAGONAL_WEIGHT = 14.5
COUPLING = 0.25
SOFTENED = 0.05

MESH = pl.DeviceIdType.MESH
F32 = jnp.float32
BF16 = jnp.bfloat16


def halves(values):
    high = values.astype(BF16)
    low = (values - high.astype(F32)).astype(BF16)
    return high, low


def onehot(matches):
    return jnp.where(matches, 1.0, 0.0).astype(BF16)


def iota(shape, dim):
    return lax.broadcasted_iota(jnp.int32, shape, dim)


def product(left, right):
    return jnp.dot(left, right, preferred_element_type=F32)


def row_index():
    return iota((ROWS, CY), 0)


def in_first_half():
    return iota((ROWS, CY), 1) < HALF


def up(slab, ends):
    first = pltpu.roll(slab[0], ROWS - 1, 0)
    turned = jnp.where(in_first_half(), pltpu.roll(first, HALF, 1), ends)
    return jnp.concatenate([slab[1:], jnp.where(row_index() == ROWS - 1, turned, first)[None]], axis=0)


def down(slab, ends):
    last = pltpu.roll(slab[PARTS - 1], 1, 0)
    turned = jnp.where(in_first_half(), ends, pltpu.roll(last, HALF, 1))
    return jnp.concatenate([jnp.where(row_index() == 0, turned, last)[None], slab[:-1]], axis=0)


def end_row(slab):
    return jnp.where(iota((1, CY), 1) < HALF, slab[0][:1], pltpu.roll(slab[PARTS - 1], 1, 0)[:1])


def turn_halves(values):
    return pltpu.roll(values, HALF, 1)


def kernel(
    nx, ny,
    owner_hbm, element_hbm, rows_hbm, modulus_hbm, birth_hbm, start_hbm, bounds_ref,
    out_ref,
    owner_ref, element_ref, rows_ref, modulus_ref, birth_ref, start_ref, in_sem,
    split_ref, place_ref, send_rows, send_ids, column_ids, got_rows, got_ids, total,
    ready_sem, column_send_sem, column_recv_sem, ids_send_sem, ids_recv_sem, rows_send_sem, rows_recv_sem,
    fields, stress, inverse, forces, born, steps, summed, differed, sliced,
    along_matrix, turning,
    packed, corner_rows, packed_stress, got_ends, got_stress_ends, ends, ends_summed, ends_differed, ends_added,
    face_send, face_recv, side_send, side_recv, corner_send, corner_recv,
    stress_face_send, stress_face_recv, stress_side_send, stress_side_recv,
):
    tiles = nx * ny
    count = rows_ref.shape[0]
    group = ny * CAP
    gx = lax.axis_index("gx")
    gy = lax.axis_index("gy")

    loads = [
        pltpu.make_async_copy(source, target, in_sem.at[i])
        for i, (source, target) in enumerate(
            [
                (owner_hbm, owner_ref), (element_hbm, element_ref), (rows_hbm, rows_ref),
                (start_hbm, start_ref), (modulus_hbm, modulus_ref), (birth_hbm, birth_ref),
            ]
        )
    ]
    for load in loads:
        load.start()

    def in_column(turn):
        return lax.rem(gx + turn, nx), gy

    def in_line(turn):
        return gx, lax.rem(gy + turn, ny)

    barrier = pltpu.get_barrier_semaphore()

    def greet_line(turn, carry):
        pl.semaphore_signal(barrier, inc=1, device_id=in_line(turn), device_id_type=MESH)
        return carry

    def greet_column(turn, carry):
        pl.semaphore_signal(barrier, inc=1, device_id=in_column(turn), device_id_type=MESH)
        return carry

    def tell_column(turn, carry):
        pl.semaphore_signal(ready_sem, inc=1, device_id=in_column(turn), device_id_type=MESH)
        return carry

    lax.fori_loop(1, ny, greet_line, 0, unroll=5)
    lax.fori_loop(1, nx, greet_column, 0)

    has = {-1: (gx > 0, gy > 0), 1: (gx < nx - 1, gy < ny - 1)}

    def present(a, b):
        if a == 0:
            return has[b][1]
        if b == 0:
            return has[a][0]
        return jnp.logical_and(has[a][0], has[b][1])

    def over(copies, do):
        for where, copy in copies:

            @pl.when(present(*where))
            def _(copy=copy):
                do(copy())

    loads[0].wait()
    loads[1].wait()
    owner = owner_ref[...]
    given = element_ref[...]
    depth_index = given // CX
    element = lax.rem(given, CX) * NZ + depth_index + 1
    member = jnp.where(iota((tiles, count), 0) == owner, 1.0, 0.0)
    member16 = member.astype(BF16)
    block = 256
    earlier = onehot(iota((block, block), 0) < iota((block, block), 1))
    carried = jnp.zeros((tiles, 1), F32)
    slots = []
    for first in range(0, count, block):
        part = member[:, first : first + block]
        before = product(member16[:, first : first + block], earlier) + carried
        slots.append(jnp.sum(before * part, axis=0, keepdims=True))
        carried = carried + jnp.sum(part, axis=1, keepdims=True)
    slot = jnp.concatenate(slots, axis=1).astype(jnp.int32)
    place_ref[...] = owner * CAP + slot

    pl.semaphore_wait(barrier, nx + ny - 2)
    lax.fori_loop(1, nx, tell_column, 0)

    loads[2].wait()
    high, low = halves(rows_ref[...])
    split_ref[:, :CY] = high
    split_ref[:, CY:] = low

    pl.semaphore_wait(ready_sem, nx - 1)

    def pack_rows(turn, carry):
        tile_x = lax.rem(gx + turn, nx)
        wanted = tile_x * group + iota((group, count), 0)
        picked = product(onehot(wanted == place_ref[...]), split_ref[...])
        send_rows[pl.ds(tile_x * ny, ny)] = (picked[:, :CY] + picked[:, CY:]).reshape(ny, CAP, CY)

        def send(turn_y, carry):
            tile_y = lax.rem(gy + turn_y, ny)
            pltpu.make_async_remote_copy(
                src_ref=send_rows.at[tile_x * ny + tile_y], dst_ref=got_rows.at[turn * ny + turn_y],
                send_sem=rows_send_sem, recv_sem=rows_recv_sem.at[turn],
                device_id=(tile_x, tile_y), device_id_type=MESH,
            ).start()
            return carry

        @pl.when(turn == 0)
        def _():
            lax.fori_loop(1, ny, send, 0, unroll=5)

        @pl.when(turn > 0)
        def _():
            lax.fori_loop(0, ny, send, 0, unroll=4)

        return carry

    lax.fori_loop(0, FIRST, pack_rows, 0)

    weighed = jnp.concatenate(
        [
            (member * (element // 32).astype(F32)).astype(BF16),
            (member * lax.rem(element, 32).astype(F32)).astype(BF16),
        ],
        axis=0,
    )
    slot_of = onehot(iota((CY, count), 0) == slot)
    both = lax.dot_general(weighed, slot_of, (((1,), (1,)), ((), ())), preferred_element_type=F32)
    send_ids[...] = (32.0 * both[:tiles] + both[tiles:]).reshape(nx, ny, 1, CY)

    def send_ids_down(turn, carry):
        to = in_column(turn)
        pltpu.make_async_remote_copy(
            src_ref=send_ids.at[to[0]], dst_ref=column_ids.at[turn],
            send_sem=column_send_sem, recv_sem=column_recv_sem,
            device_id=to, device_id_type=MESH,
        ).start()
        return carry

    lax.fori_loop(1, nx, send_ids_down, 0)
    column_ids[0] = send_ids[gx]

    def send_ids_along(turn, carry):
        to = in_line(turn)
        pltpu.make_async_remote_copy(
            src_ref=column_ids.at[:, to[1]], dst_ref=got_ids.at[:, turn],
            send_sem=ids_send_sem, recv_sem=ids_recv_sem,
            device_id=to, device_id_type=MESH,
        ).start()
        return carry

    zeros = jnp.zeros((ROWS, CY), F32)
    corner_rows[...] = jnp.zeros_like(corner_rows)
    for hand, slab_at, group_at in ((-1, 0, 0), (1, CX + 1, 3)):

        @pl.when(jnp.logical_not(has[hand][0]))
        def _(slab_at=slab_at, group_at=group_at):
            stress[slab_at] = jnp.zeros(SLAB, F32)
            for sweep in range(SWEEPS):
                for c in range(3):
                    fields[sweep, c, slab_at] = jnp.zeros(SLAB, F32)
                    for side_at in range(2):
                        got_ends[sweep, side_at, c, group_at] = zeros

        @pl.when(jnp.logical_not(has[hand][1]))
        def _(side_at=(hand + 1) // 2):
            got_stress_ends[side_at] = jnp.zeros((2, ROWS, CY), F32)
            for sweep in range(SWEEPS):
                for c in range(3):
                    got_ends[sweep, side_at, c] = jnp.zeros((4, ROWS, CY), F32)

    row, column = iota((2 * CY, 2 * CY), 0), iota((2 * CY, 2 * CY), 1)
    k, z = lax.rem(row, CY), lax.rem(column, CY)
    off = jnp.where(k // NZ == z // NZ, k - z, 2)
    after, before = jnp.where(off == 1, 1.0, 0.0), jnp.where(off == -1, 1.0, 0.0)
    sums = jnp.where(off == 0, 2.0, after + before)
    along_matrix[...] = jnp.where(column < CY, sums, after - before).astype(BF16)

    first_half = iota((2 * NZ // 2, CY), 1) < HALF

    def slabs_of(pair, at):
        turned = pair.T
        begin, end = turned[:NZ], turned[NZ:]
        slabs = []
        for odd, values in enumerate(
            (jnp.where(first_half, begin, turn_halves(end)), jnp.where(first_half, turn_halves(begin), end))
        ):
            turning[2 * at + odd] = values
            slabs.append(jnp.stack([turning[2 * at + odd, pl.ds(part, ROWS, stride=PARTS), :] for part in range(PARTS)]))
        return slabs

    def pair_of_slabs(slabs, at):
        for odd in range(2):
            for part in range(PARTS):
                turning[2 * at + odd, pl.ds(part, ROWS, stride=PARTS), :] = slabs[odd][part]
        even, odd = turning[2 * at], turning[2 * at + 1]
        return jnp.concatenate(
            [jnp.where(first_half, even, turn_halves(odd)), jnp.where(first_half, turn_halves(even), odd)], axis=0
        ).T

    def over_pairs(body):
        def some(i, carry):
            for at in range(TOGETHER):
                body(TOGETHER * i + at, 3 * at)
            return carry

        lax.fori_loop(0, CX // 2 // TOGETHER, some, 0)

    def rows_of(x, part):
        return pl.ds(part * ROWS * CX + x, ROWS, stride=CX)

    def take(ref, i):
        return jnp.concatenate([ref[rows_of(2 * i + odd, part), :] for odd in range(2) for part in range(NZ // ROWS)], axis=0)

    def slice_up(slab, at):
        high, low = halves(slab.reshape(NZ, CY))
        sliced[at, :, :CY] = high
        sliced[at, :, CY:] = low

    def merge_ends(from_left, from_right):
        return turn_halves(jnp.where(in_first_half(), from_right, from_left))

    def face(sweep, a):
        mine, theirs = (1, CX + 1) if a < 0 else (CX, 0)
        return pltpu.make_async_remote_copy(
            src_ref=fields.at[sweep, :, mine], dst_ref=fields.at[sweep, :, theirs],
            send_sem=face_send.at[sweep, (a + 1) // 2], recv_sem=face_recv.at[sweep, (1 - a) // 2],
            device_id=(gx + a, gy), device_id_type=MESH,
        )

    def side(sweep, b):
        return pltpu.make_async_remote_copy(
            src_ref=packed.at[sweep], dst_ref=got_ends.at[sweep, (1 - b) // 2, :, pl.ds(1, 2)],
            send_sem=side_send.at[sweep, (b + 1) // 2], recv_sem=side_recv.at[sweep, (1 - b) // 2],
            device_id=(gx, gy + b), device_id_type=MESH,
        )

    def corner(sweep, a, b):
        mine, theirs = (0, 3) if a < 0 else (1, 0)
        return pltpu.make_async_remote_copy(
            src_ref=corner_rows.at[sweep, :, mine], dst_ref=got_ends.at[sweep, (1 - b) // 2, :, theirs],
            send_sem=corner_send.at[sweep, a + 1 + (b + 1) // 2], recv_sem=corner_recv.at[sweep, 1 - a + (1 - b) // 2],
            device_id=(gx + a, gy + b), device_id_type=MESH,
        )

    def stress_face(a):
        mine, theirs = (1, CX + 1) if a < 0 else (CX, 0)
        return pltpu.make_async_remote_copy(
            src_ref=stress.at[mine], dst_ref=stress.at[theirs],
            send_sem=stress_face_send.at[(a + 1) // 2], recv_sem=stress_face_recv.at[(1 - a) // 2],
            device_id=(gx + a, gy), device_id_type=MESH,
        )

    def stress_side(b):
        return pltpu.make_async_remote_copy(
            src_ref=packed_stress, dst_ref=got_stress_ends.at[(1 - b) // 2],
            send_sem=stress_side_send.at[(b + 1) // 2], recv_sem=stress_side_recv.at[(1 - b) // 2],
            device_id=(gx, gy + b), device_id_type=MESH,
        )

    pair_of = (-1, 1)

    def faces(sweep):
        return [((a, 0), lambda a=a: face(sweep, a)) for a in pair_of]

    def sides(sweep):
        return [((0, b), lambda b=b: side(sweep, b)) for b in pair_of]

    def corners(sweep):
        return [((a, b), lambda a=a, b=b: corner(sweep, a, b)) for a in pair_of for b in pair_of]

    stress_faces = [((a, 0), lambda a=a: stress_face(a)) for a in pair_of]
    stress_sides = [((0, b), lambda b=b: stress_side(b)) for b in pair_of]

    def arrival(ref, sem):
        return lambda: pltpu.make_async_copy(ref, ref, sem)

    def from_faces(sweep):
        return [
            ((a, 0), arrival(fields.at[sweep, :, 0 if a < 0 else CX + 1], face_recv.at[sweep, (a + 1) // 2]))
            for a in pair_of
        ]

    def from_edges(sweep):
        return [
            ((0, b), arrival(got_ends.at[sweep, (b + 1) // 2, :, pl.ds(1, 2)], side_recv.at[sweep, (b + 1) // 2]))
            for b in pair_of
        ] + [
            (
                (a, b),
                arrival(
                    got_ends.at[sweep, (b + 1) // 2, :, 0 if a < 0 else 3],
                    corner_recv.at[sweep, a + 1 + (b + 1) // 2],
                ),
            )
            for a in pair_of
            for b in pair_of
        ]

    from_stress_faces = [
        ((a, 0), arrival(stress.at[0 if a < 0 else CX + 1], stress_face_recv.at[(a + 1) // 2])) for a in pair_of
    ]
    from_stress_sides = [
        ((0, b), arrival(got_stress_ends.at[(b + 1) // 2], stress_side_recv.at[(b + 1) // 2])) for b in pair_of
    ]

    def start(copy):
        copy.start()

    def receive(copy):
        copy.wait()

    def finish(copy):
        copy.wait_send()

    def along_own(sweep):
        for c in range(3):
            at = pl.ds(c * SLABS + 1, CX)
            both = product(sliced[at].reshape(CX * NZ, 2 * CY), along_matrix[...])
            summed[at] = both[:, :CY].reshape((CX,) + SLAB)
            differed[at] = both[:, CY:].reshape((CX,) + SLAB)

    def along_halo(sweep):
        over(from_edges(sweep) + from_faces(sweep), receive)
        for c in range(3):
            for g in range(4):
                at = pl.ds(g * ROWS, ROWS)
                ends[c, at] = merge_ends(got_ends[sweep, 0, c, g], got_ends[sweep, 1, c, g])
        halo = [fields[sweep, c, at].reshape(NZ, CY) for c in range(3) for at in (0, CX + 1)]
        high, low = halves(jnp.concatenate(halo + [ends[c] for c in range(3)], axis=0))
        both = product(jnp.concatenate([high, low], axis=1), along_matrix[...])
        for c in range(3):
            for hand, at in enumerate((0, CX + 1)):
                first = (2 * c + hand) * NZ
                summed[c * SLABS + at] = both[first : first + NZ, :CY].reshape(SLAB)
                differed[c * SLABS + at] = both[first : first + NZ, CY:].reshape(SLAB)
            first = 6 * NZ + c * 4 * ROWS
            ends_summed[c] = both[first : first + 4 * ROWS, :CY]
            ends_differed[c] = both[first : first + 4 * ROWS, CY:]

        def near(ref, c, step):
            return ref[c, pl.ds(ROWS + step, CX), :]

        for c in range(3):
            around = (near(ends_summed, c, -1) + near(ends_summed, c, 1)) + 2.0 * near(ends_summed, c, 0)
            if c == 0:
                across = near(ends_differed, 2, 0)
            elif c == 1:
                across = near(ends, 2, 1) - near(ends, 2, -1)
            else:
                across = near(ends_differed, 0, 0) + (near(ends, 1, 1) - near(ends, 1, -1))
            sign = jnp.where(iota((CX, CY), 1) < HALF, -COUPLING, COUPLING)
            ends_added[c] = around + sign * across

    def rest(sweep, x, c):
        at = x + 1

        def field(component, to):
            return fields[sweep, component, to]

        def along_sum(to):
            return summed[c * SLABS + to]

        def along_difference(component, to):
            return differed[component * SLABS + to]

        around = (along_sum(at - 1) + along_sum(at + 1)) + 2.0 * along_sum(at)
        if c == 0:
            across = along_difference(2, at)
        elif c == 1:
            across = field(2, at + 1) - field(2, at - 1)
        else:
            across = along_difference(0, at) + (field(1, at + 1) - field(1, at - 1))
        across = COUPLING * across
        added = ends_added[c, pl.ds(x, 1), :]
        total_around = (up(around + across, added) + down(around - across, added)) + 2.0 * around
        if c < 2:
            total_around = total_around + COUPLING * (along_difference(1 - c, at + 1) - along_difference(1 - c, at - 1))
        return (0.25 / DIAGONAL_WEIGHT) * total_around - ((DIAGONAL_WEIGHT + 2.0) / DIAGONAL_WEIGHT) * field(c, at)

    loads[3].wait()

    def store_ends(slab, x, ref):
        ref[x // ROWS, pl.ds(lax.rem(x, ROWS), 1), :] = end_row(slab)

    def keep_corners(sweep, which):
        row = pl.ds((ROWS - 1) * which, 1)
        for c in range(3):
            corner_rows[sweep, c, which, row, :] = packed[sweep, c, which, row, :]

    def begin(i, room):
        for c in range(3):
            for odd, slab in enumerate(slabs_of(take(start_ref.at[c], i), room + c)):
                x = 2 * i + odd
                fields[0, c, x + 1] = slab
                slice_up(slab, c * SLABS + x + 1)
                store_ends(slab, x, packed.at[0, c])

    over_pairs(begin)
    for which in range(2):
        keep_corners(0, which)
    over(corners(0) + sides(0) + faces(0), start)
    lax.fori_loop(FIRST, SECOND, pack_rows, 0)
    from_column = pl.ds(1, nx - 1)
    pltpu.make_async_copy(column_ids.at[from_column], column_ids.at[from_column], column_recv_sem).wait()
    lax.fori_loop(1, ny, send_ids_along, 0)
    got_ids[:, 0] = column_ids[:, gy]
    lax.fori_loop(SECOND, nx, pack_rows, 0)
    got_rows[0] = send_rows[gx * ny + gy]

    loads[4].wait()
    loads[5].wait()

    def material(i, room):
        for odd, modulus in enumerate(slabs_of(take(modulus_ref, i), room)):
            x = 2 * i + odd
            stress[x + 1] = modulus
            inverse[x] = 1.0 / (DIAGONAL_WEIGHT * modulus)
        for odd, birth in enumerate(slabs_of(take(birth_ref, i).astype(F32), room + 1)):
            born[2 * i + odd] = birth

    over_pairs(material)
    along_own(0)

    lower = jnp.full((ROWS, CY), bounds_ref[0], F32)
    upper = jnp.full((ROWS, CY), bounds_ref[1], F32)
    theta = (upper + lower) / 2.0
    delta = (upper - lower) / 2.0
    sigma = theta / delta
    ratio = 1.0 / sigma

    along_halo(0)

    def first_rest(x, carry):
        for c in range(3):
            steps[c, x] = rest(0, x, c)
        return carry

    lax.fori_loop(0, CX, first_rest, 0, unroll=4)

    others = pl.ds(1, tiles - 1)
    from_line = pl.ds(1, ny - 1)
    pltpu.make_async_copy(got_ids.at[:, from_line], got_ids.at[:, from_line], ids_recv_sem).wait()
    spread = onehot(iota((CY, group), 0) == lax.rem(iota((CY, group), 1), CAP))
    own_lane = iota((ny, group), 0) == iota((ny, group), 1) // CAP
    total[...] = jnp.zeros_like(total)

    def collect(turn, carry):
        @pl.when(turn == 0)
        def _():
            part = got_rows.at[pl.ds(1, ny - 1)]
            pltpu.make_async_copy(part, part, rows_recv_sem.at[0]).wait()

        @pl.when(turn > 0)
        def _():
            part = got_rows.at[pl.ds(turn * ny, ny)]
            pltpu.make_async_copy(part, part, rows_recv_sem.at[turn]).wait()

        part = got_rows.at[pl.ds((turn + 1) * ny, ny)]
        pltpu.make_async_copy(part, part, rows_recv_sem.at[turn + 1]).wait()
        places = []
        for at in range(2):
            ids = got_ids[turn + at].reshape(ny, CY)
            ids_high = jnp.floor(ids * (1.0 / 32.0))
            ids_low = ids - 32.0 * ids_high
            wide = 32.0 * product(ids_high.astype(BF16), spread) + product(ids_low.astype(BF16), spread)
            flat = jnp.sum(jnp.where(own_lane, wide, 0.0), axis=0, keepdims=True).astype(jnp.int32) - 1
            places.append(onehot(iota((CELLS, group), 0) == flat))
        high, low = halves(got_rows[pl.ds(turn * ny, 2 * ny)].reshape(2 * group, CY))
        total[...] += product(jnp.concatenate(places, axis=1), jnp.concatenate([high, low], axis=1))
        return carry

    lax.fori_loop(0, nx // 2, lambda pair, carry: collect(2 * pair, carry), 0)

    def strain(i, room):
        at = pl.ds(2 * i * NZ, 2 * NZ)
        for odd, slab in enumerate(slabs_of(total[at, :CY] + total[at, CY:], room)):
            x = 2 * i + odd
            slab = stress[x + 1] * slab
            stress[x + 1] = slab
            slice_up(slab, x + 1)
            store_ends(slab, x, packed_stress)

    strain(0, 0)
    strain(CX // 2 - 1, 3)
    over(stress_faces, start)

    def strain_inner(k, carry):
        for at in range(3):
            strain(1 + 3 * k + at, 3 * at)
        return carry

    lax.fori_loop(0, 2, strain_inner, 0)
    over(stress_sides, start)
    at = pl.ds(1, CX)
    differed[at] = product(sliced[at].reshape(CX * NZ, 2 * CY), along_matrix[:, CY:]).reshape((CX,) + SLAB)
    over(from_stress_sides, receive)
    for g in range(2):
        ends[0, pl.ds(g * ROWS, ROWS)] = merge_ends(got_stress_ends[0, g], got_stress_ends[1, g])
    over(from_stress_faces, receive)

    def keep_moved(sweep, x, c, moved, step):
        at = x + 1
        steps[c, x] = step
        fields[sweep + 1, c, at] = moved
        slice_up(moved, c * SLABS + at)
        store_ends(moved, x, packed.at[sweep + 1, c])

    def softer(sweep, x):
        return jnp.where(born[x] <= sweep, 1.0, 1.0 / SOFTENED)

    first_gain = 1.0 / theta

    def first_move(x):
        middle = stress[x + 1]
        scale = 0.5 * inverse[x]
        soft = softer(0, x)
        added = ends[0, pl.ds(x, 1), :]
        gradients = (differed[x + 1], stress[x + 2] - stress[x], up(middle, added) - down(middle, added))
        for c, gradient in enumerate(gradients):
            force = scale * gradient
            forces[c, x] = force
            step = first_gain * (steps[c, x] + soft * force)
            keep_moved(0, x, c, fields[0, c, x + 1] + step, step)

    def ends_first(move, sweep):
        lax.fori_loop(0, 2, lambda i, carry: (move(i * (CX - 1)), carry)[1], 0, unroll=2)
        for which in range(2):
            keep_corners(sweep + 1, which)
        over(corners(sweep + 1) + faces(sweep + 1), start)
        lax.fori_loop(1, CX - 1, lambda x, carry: (move(x), carry)[1], 0, unroll=2)
        over(sides(sweep + 1), start)
        along_own(sweep + 1)

    ends_first(first_move, 0)

    for sweep in range(1, SWEEPS):
        ratio_next = 1.0 / (2.0 * sigma - ratio)
        keep = ratio_next * ratio
        gain = 2.0 * ratio_next / delta
        ratio = ratio_next
        along_halo(sweep)

        def moves(x, sweep=sweep, keep=keep, gain=gain):
            soft = softer(sweep, x)
            for c in range(3):
                step = gain * (rest(sweep, x, c) + soft * forces[c, x]) + keep * steps[c, x]
                yield c, fields[sweep, c, x + 1] + step, step

        if sweep < SWEEPS - 1:

            def move(x, sweep=sweep, moves=moves):
                for c, moved, step in moves(x):
                    keep_moved(sweep, x, c, moved, step)

            ends_first(move, sweep)
        else:

            def last(i, room, moves=moves):
                both = [[moved for _, moved, _ in moves(2 * i + odd)] for odd in range(2)]
                for c in range(3):
                    block = pair_of_slabs([both[0][c], both[1][c]], room + c)
                    for odd in range(2):
                        for part in range(NZ // ROWS):
                            first = odd * NZ + part * ROWS
                            out_ref[c, rows_of(2 * i + odd, part), :] = block[first : first + ROWS]

            over_pairs(last)

    pltpu.make_async_copy(column_ids.at[from_column], column_ids.at[from_column], column_send_sem).wait()
    pltpu.make_async_copy(got_ids.at[:, from_line], got_ids.at[:, from_line], ids_send_sem).wait()
    pltpu.make_async_copy(send_rows.at[others], send_rows.at[others], rows_send_sem).wait()
    over(stress_faces + stress_sides, finish)
    for sweep in range(SWEEPS):
        over(corners(sweep) + sides(sweep) + faces(sweep), finish)


def local(thermal_rows, row_owner, row_element, modulus, birth, start_disp, bounds):
    nx, ny = lax.axis_size("gx"), lax.axis_size("gy")
    tiles = nx * ny
    count = thermal_rows.shape[0]
    vmem, dma = pltpu.VMEM, pltpu.SemaphoreType.DMA
    moved = pl.pallas_call(
        functools.partial(kernel, nx, ny),
        out_shape=jax.ShapeDtypeStruct((3, CELLS, CY), F32),
        in_specs=[pl.BlockSpec(memory_space=pltpu.HBM)] * 6 + [pl.BlockSpec(memory_space=pltpu.SMEM)],
        out_specs=pl.BlockSpec(memory_space=pltpu.VMEM),
        scratch_shapes=[
            vmem((1, count), jnp.int32),
            vmem((1, count), jnp.int32),
            vmem((count, CY), F32),
            vmem((CELLS, CY), F32),
            vmem((CELLS, CY), jnp.int32),
            vmem((3, CELLS, CY), F32),
            dma((6,)),
            vmem((count, 2 * CY), BF16),
            vmem((1, count), jnp.int32),
            vmem((tiles, CAP, CY), F32),
            vmem((nx, ny, 1, CY), F32),
            vmem((nx, ny, 1, CY), F32),
            vmem((tiles, CAP, CY), F32),
            vmem((nx, ny, 1, CY), F32),
            vmem((CELLS, 2 * CY), F32),
            pltpu.SemaphoreType.REGULAR,
            dma, dma, dma, dma, dma, dma((nx,)),
            vmem((SWEEPS, 3, SLABS) + SLAB, F32),
            vmem((SLABS,) + SLAB, F32),
            vmem((CX,) + SLAB, F32),
            vmem((3, CX) + SLAB, F32),
            vmem((CX,) + SLAB, F32),
            vmem((3, CX) + SLAB, F32),
            vmem((3 * SLABS,) + SLAB, F32),
            vmem((3 * SLABS,) + SLAB, F32),
            vmem((3 * SLABS, NZ, 2 * CY), BF16),
            vmem((2 * CY, 2 * CY), BF16),
            vmem((6 * TOGETHER, NZ, CY), F32),
            vmem((SWEEPS, 3, 2, ROWS, CY), F32),
            vmem((SWEEPS, 3, 2, ROWS, CY), F32),
            vmem((2, ROWS, CY), F32),
            vmem((SWEEPS, 2, 3, 4, ROWS, CY), F32),
            vmem((2, 2, ROWS, CY), F32),
            vmem((3, 4 * ROWS, CY), F32),
            vmem((3, 4 * ROWS, CY), F32),
            vmem((3, 4 * ROWS, CY), F32),
            vmem((3, CX, CY), F32),
            dma((SWEEPS, 2)), dma((SWEEPS, 2)), dma((SWEEPS, 2)), dma((SWEEPS, 2)), dma((SWEEPS, 4)), dma((SWEEPS, 4)),
            dma((2,)), dma((2,)), dma((2,)), dma((2,)),
        ],
        compiler_params=pltpu.CompilerParams(
            collective_id=0, has_side_effects=True, vmem_limit_bytes=60 * 1024 * 1024
        ),
        name="weld",
    )(
        row_owner.reshape(1, count), row_element.reshape(1, count), thermal_rows,
        modulus.reshape(CELLS, CY), birth.reshape(CELLS, CY), start_disp.reshape(3, CELLS, CY), bounds,
    )
    return moved.reshape(start_disp.shape)


def solution(mesh):
    placed = (
        P(("gx", "gy"), None),
        P(("gx", "gy"), None),
        P(("gx", "gy"), None),
        P(None, "gx", "gy"),
        P(None, "gx", "gy"),
        P(None, None, "gx", "gy"),
        P(),
    )
    return jax.shard_map(
        local, mesh=mesh, in_specs=placed, out_specs=P(None, None, "gx", "gy"), check_vma=False
    )
```
